512 devices in a mesh: xy: 64 (over y, z), gz: 8 (over x, core).
Axes of the slice: x: 4, y: 4, z: 16, core: 2. Of those that a mesh axis runs over, the one named last changes fastest.
Arguments:
- conc_prev: float32 [4, 16, 1024, 1024], P(None, 'gz', 'xy'), may hold values from 0.5 to 2
- conc_section: float32 [3, 4, 16, 1024, 1024], P(None, None, 'gz', 'xy'), may hold values from 0.5 to 2
- potential: float32 [3, 16, 1024, 1024], P(None, 'gz', 'xy'), may hold values from -6 to 6
- diffusivity: float32 [4], replicated, may hold values from 0.2 to 1
- charges: int32 [4], replicated, may hold values from -2 to 2, as said below
Outputs:
- conc_new: float32 [3, 4, 16, 1024, 1024], P(None, None, 'gz', 'xy')
- potential_new: float32 [3, 16, 1024, 1024], P(None, 'gz', 'xy')
The draws below stay inside these ranges and needn't reach their ends.
Inputs may be any that keep to these rules, and one draw needn't show every extreme that they name: Each charge is plus or minus 1 or 2, and the 4 charges sum to zero.
All inputs are finite; a program needn't handle non-finite values.
Results may differ from the reference program's by a relative error of at most 0.00027.
Values sent between devices are 32-bit elements; how exact they have to be, the bound alone decides.
No kernel may reach another device: no remote copies, remote signals or barrier semaphores. Data moves between devices by JAX's collectives and lax.ppermute only.
A program may use at most 64 MiB of HBM per device.

```python
import math
import jax
import jax.numpy as jnp
from jax import lax

NX = 1024
NY = 1024
SPECIES = 4
SECTIONS = 3
NZ = 16


def draw_charges(key, part):
    key = jax.random.fold_in(key, 11)
    first_key, order_key = jax.random.split(key)
    second = jax.random.randint(first_key, (1,), 1, 3).astype(jnp.int32)
    magnitude = jnp.concatenate([jnp.full((1,), 2, jnp.int32), second])
    values = jnp.concatenate([magnitude, -magnitude])
    return jax.random.permutation(order_key, values).astype(jnp.int32)


def steps_of(rng, dims, cuts, least, largest):
    def one(axis_at, parts):
        draws = jax.random.uniform(jax.random.fold_in(jax.random.fold_in(rng, 6), axis_at), (parts,), jnp.float32, least / len(cuts), largest / len(cuts))
        return jnp.repeat(jnp.exp(draws), dims[axis_at] // parts).reshape((-1,) + (1,) * (len(dims) - axis_at - 1))

    factor_of = one(*cuts[0])
    for cut in cuts[1:]:
        factor_of = factor_of * one(*cut)
    return factor_of


def noise(key, extent, scale, reach, cuts=(), kind=jnp.bfloat16):
    array = scale * jax.random.normal(key, extent, jnp.float32)
    if cuts:
        array = array * steps_of(key, extent, cuts, -0.22, 0.18)
    return jnp.clip(array, -reach, reach).astype(kind)


def setup_inputs(seed: int = 0) -> dict:
    arg_keys = jax.random.split(jax.random.key(seed), 6)
    return {
        "conc_prev": jnp.clip(jnp.exp(math.log(2.0) - 1.3862944 * jax.random.uniform(arg_keys[0], (SPECIES, NZ, NX, NY), jnp.float32) ** steps_of(arg_keys[0], (SPECIES, NZ, NX, NY), ((1, 8), (2, 64)), -0.2, 0.2)), 0.5, 2.0),
        "conc_section": jnp.clip(jnp.exp(math.log(2.0) - 1.3862944 * jax.random.uniform(arg_keys[1], (SECTIONS, SPECIES, NZ, NX, NY), jnp.float32) ** steps_of(arg_keys[1], (SECTIONS, SPECIES, NZ, NX, NY), ((2, 8), (3, 64)), -0.2, 0.2)), 0.5, 2.0),
        "potential": noise(arg_keys[2], (SECTIONS, NZ, NX, NY), 1.0, 6.0, ((1, 8), (2, 64)), jnp.float32),
        "diffusivity": jnp.clip(jnp.exp(jax.random.uniform(arg_keys[3], (SPECIES,), jnp.float32, math.log(0.2), math.log(1.0))), 0.2, 1.0),
        "charges": draw_charges(jax.random.fold_in(arg_keys[5], 71), 0),
    }


step_size = 0.2
screening = 0.005

def radau_matrix():
    root = math.sqrt(6.0)
    return [[(88.0 - 7.0 * root) / 360.0, (296.0 - 169.0 * root) / 1800.0, (-2.0 + 3.0 * root) / 225.0], [(296.0 + 169.0 * root) / 1800.0, (88.0 + 7.0 * root) / 360.0, (-2.0 - 3.0 * root) / 225.0], [(16.0 - root) / 36.0, (16.0 + root) / 36.0, 1.0 / 9.0]]

def shifted(field):
    zero_layer = jnp.zeros_like(field[:1])
    z_pair = (jnp.concatenate([field[1:], zero_layer], 0), jnp.concatenate([zero_layer, field[:-1]], 0))
    x_pair = (jnp.roll(field, -1, 1), jnp.roll(field, 1, 1))
    y_pair = (jnp.roll(field, -1, 2), jnp.roll(field, 1, 2))
    return [z_pair, x_pair, y_pair]

def drift_term(conc_plus, conc_minus, pot_plus, pot_minus, conc, pot, charge):
    return conc_plus - conc + charge * 0.5 * (conc_plus + conc) * (pot_plus - pot) - (conc - conc_minus) - charge * 0.5 * (conc + conc_minus) * (pot - pot_minus)

def thomas(rhs, diag):

    def forward(carry, row):
        c_prev, d_prev = carry
        inverse = 1.0 / (diag - c_prev)
        d_next = (row - d_prev) * inverse
        return ((inverse, d_next), (inverse, d_next))
    init = (jnp.zeros_like(diag), jnp.zeros_like(rhs[0]))
    _, (c_rows, d_rows) = lax.scan(forward, init, rhs)

    def backward(x_next, pair):
        x_here = pair[1] - pair[0] * x_next
        return (x_here, x_here)
    _, solved = lax.scan(backward, jnp.zeros_like(rhs[0]), (c_rows, d_rows), reverse=True)
    return solved

def reference(conc_prev, conc_section, potential, diffusivity, charges):
    butcher = radau_matrix()
    charge_f = charges.astype(jnp.float32)
    pot_shifts = [shifted(potential[section_j]) for section_j in range(SECTIONS)]
    fluxes = []
    for section_j in range(SECTIONS):
        row = []
        for species in range(SPECIES):
            conc = conc_section[section_j, species]
            total = jnp.zeros_like(conc)
            for (conc_plus, conc_minus), (pot_plus, pot_minus) in zip(shifted(conc), pot_shifts[section_j]):
                total = total + drift_term(conc_plus, conc_minus, pot_plus, pot_minus, conc, potential[section_j], charge_f[species])
            row.append(diffusivity[species] * total)
        fluxes.append(row)
    ex = 2.0 * jnp.cos(jnp.arange(NX).astype(jnp.float32) * (2.0 * math.pi / NX)) - 2.0
    ey = 2.0 * jnp.cos(jnp.arange(NY).astype(jnp.float32) * (2.0 * math.pi / NY)) - 2.0
    diag = ex[:, None] + ey[None, :] - 2.0 - screening
    conc_out = []
    pot_out = []
    for section_i in range(SECTIONS):
        species_out = []
        density = jnp.zeros_like(potential[0])
        for species in range(SPECIES):
            combined = butcher[section_i][0] * fluxes[0][species] + butcher[section_i][1] * fluxes[1][species] + butcher[section_i][2] * fluxes[2][species]
            resid = conc_section[section_i, species] - conc_prev[species] - step_size * combined
            updated = conc_section[section_i, species] - resid / (1.0 + 6.0 * step_size * butcher[section_i][section_i] * diffusivity[species])
            species_out.append(updated)
            density = density + charge_f[species] * updated
        conc_out.append(jnp.stack(species_out))
        pot = potential[section_i]
        laplace = jnp.zeros_like(pot)
        for pot_plus, pot_minus in pot_shifts[section_i]:
            laplace = laplace + (pot_plus + pot_minus - 2.0 * pot)
        rhs = -(laplace + density)
        spectrum = jnp.fft.fft2(rhs, axes=(1, 2))
        solved = thomas(spectrum, diag)
        delta = jnp.fft.ifft2(solved, axes=(1, 2)).real.astype(jnp.float32)
        pot_out.append(pot + delta)
    return (jnp.stack(conc_out), jnp.stack(pot_out))
```

```python
import math

import jax
import jax.numpy as jnp
import numpy as np
from jax import lax
from jax.experimental import pallas as pl
from jax.experimental.pallas import tpu as pltpu
from jax.sharding import PartitionSpec as P

step_size = 0.2
screening = 0.005
lanes = 128


def radau_matrix():
    root = math.sqrt(6.0)
    return [
        [(88.0 - 7.0 * root) / 360.0, (296.0 - 169.0 * root) / 1800.0, (-2.0 + 3.0 * root) / 225.0],
        [(296.0 + 169.0 * root) / 1800.0, (88.0 + 7.0 * root) / 360.0, (-2.0 - 3.0 * root) / 225.0],
        [(16.0 - root) / 36.0, (16.0 + root) / 36.0, 1.0 / 9.0],
    ]


def cas_halves(length, scale):
    index = np.arange(length)
    angle = (index[:, None] * index[None, :] % length) * (2.0 * math.pi / length)
    table = ((np.cos(angle) + np.sin(angle)) * scale).astype(np.float32)
    high = table.astype(jnp.bfloat16)
    low = (table - high.astype(np.float32)).astype(jnp.bfloat16)
    return high, low


def sine_matrix(depth):
    k = np.arange(1, depth + 1)
    return math.sqrt(2.0 / (depth + 1)) * np.sin(np.outer(k, k) * math.pi / (depth + 1))


def decay_tables(depth, y_cells, x_cells, block):
    ez = 2.0 - 2.0 * np.cos(np.arange(1, depth + 1) * math.pi / (depth + 1))
    ey = 2.0 - 2.0 * np.cos(np.arange(y_cells) * 2.0 * math.pi / y_cells)
    lam = screening + ez[:, None] + ey[None, :]
    root = np.sqrt(lam + 0.25 * lam * lam)
    r = 1.0 / (1.0 + 0.5 * lam + root)
    return np.stack([r, 0.5 / root, r**block, 1.0 / (1.0 - r**x_cells)]).astype(np.float32)


def face(near, far, gain):
    return (far - near) + gain * (near + far)


def split_dot(rows, high_ref, low_ref):
    high = rows.astype(jnp.bfloat16)
    low = (rows - high.astype(jnp.float32)).astype(jnp.bfloat16)

    def product(a, b):
        return jnp.dot(a, b, preferred_element_type=jnp.float32)

    return product(high, low_ref[...]) + product(low, high_ref[...]) + product(high, high_ref[...])


def inner_kernel(coef_ref, inv_ref, half_ref, prev_ref, conc_ref, pot_ref, left_ref, right_ref, out_ref):
    n_section, n_species, depth, rows, y_cells = conc_ref.shape
    row = lax.broadcasted_iota(jnp.int32, (rows, y_cells), 0)

    def species(s, carry):
        half = half_ref[s]
        totals = []
        for j in range(n_section):
            planes = []
            for z in range(depth):
                c = conc_ref[j, s, z]
                p = pot_ref[j, z]
                edge = left_ref[j, s, z]
                edge_p = left_ref[j, n_species, z]
                c_before = jnp.where(row == 0, edge, pltpu.roll(c, 1, 0))
                p_before = jnp.where(row == 0, edge_p, pltpu.roll(p, 1, 0))
                low = face(c_before, c, half * (p - p_before))
                c_last = c[rows - 1 :]
                p_last = p[rows - 1 :]
                last = face(
                    c_last, right_ref[j, s, z], half * (right_ref[j, n_species, z] - p_last)
                )
                high = jnp.where(row == rows - 1, last, pltpu.roll(low, rows - 1, 0))
                c_next = pltpu.roll(c, y_cells - 1, 1)
                p_next = pltpu.roll(p, y_cells - 1, 1)
                ahead = face(c, c_next, half * (p_next - p))
                planes.append((high - low) + (ahead - pltpu.roll(ahead, 1, 1)))
            between = face(conc_ref[j, s, 0], conc_ref[j, s, 1], half * (pot_ref[j, 1] - pot_ref[j, 0]))
            totals.append((planes[0] + between, planes[1] - between))
        for z in range(depth):
            for i in range(n_section):
                c = conc_ref[i, s, z]
                update = inv_ref[i * n_species + s] * (prev_ref[s, z] - c)
                for j in range(n_section):
                    update = update + coef_ref[(i * n_section + j) * n_species + s] * totals[j][z]
                out_ref[i, s, z] = c + update
        return carry

    lax.fori_loop(0, n_species, species, 0)


def outer_kernel(
    coef_ref, half_ref, part_ref, conc_ref, pot_ref, below_ref, above_ref, high_ref, low_ref,
    out_ref, modes_ref, rhs_ref,
):
    n_section, n_species, depth, rows, y_cells = conc_ref.shape
    for i in range(n_section):
        for z in range(depth):
            rhs_ref[i, z] = screening * pot_ref[i, z]

    def species(s, carry):
        half = half_ref[s]
        for z in range(depth):
            faces = []
            for j in range(n_section):
                c = conc_ref[j, s, z]
                p = pot_ref[j, z]
                if z == 0:
                    far, far_p = below_ref[j, s], below_ref[j, n_species]
                else:
                    far, far_p = above_ref[j, s], above_ref[j, n_species]
                faces.append(face(c, far, half * (far_p - p)))
            for i in range(n_section):
                update = part_ref[i, s, z]
                for j in range(n_section):
                    update = update + coef_ref[(i * n_section + j) * n_species + s] * faces[j]
                out_ref[i, s, z] = update
                rhs_ref[i, z] += (2.0 * half) * update
        return carry

    lax.fori_loop(0, n_species, species, 0)
    rhs = rhs_ref[...].reshape(n_section * depth * rows, y_cells)
    modes = split_dot(rhs, high_ref, low_ref)
    for g in range(y_cells // lanes):
        modes_ref[g] = modes[:, g * lanes : (g + 1) * lanes].reshape(n_section, depth, rows, lanes)


def sine_rows(planes, table):
    depth = len(planes)
    half = depth // 2
    even = [planes[z] + planes[depth - 1 - z] for z in range(half)]
    odd = [planes[z] - planes[depth - 1 - z] for z in range(half)]
    out = []
    for k in range(depth):
        source = even if k % 2 == 0 else odd
        total = source[0] * float(table[k, 0])
        for z in range(1, half):
            total = total + source[z] * float(table[k, z])
        out.append(total)
    return out


def sum_kernel(table, decay_ref, modes_ref, hat_ref, sums_ref, rows_ref):
    n_gz, n_section, n_z, rows, _ = modes_ref.shape
    depth = n_gz * n_z
    r = decay_ref[0]
    sums_ref[...] = jnp.zeros_like(sums_ref)
    for i in range(n_section):
        planes = [modes_ref[z // n_z, i, z % n_z] for z in range(depth)]
        for k, plane in enumerate(sine_rows(planes, table)):
            rows_ref[i, pl.ds(k * rows, rows), :] = plane
        for x in range(rows):
            hat_ref[i, x] = rows_ref[i, pl.ds(x, depth, stride=rows), :]
        ahead = hat_ref[i, 0]
        back = hat_ref[i, rows - 1]
        for x in range(1, rows):
            ahead = ahead * r + hat_ref[i, x]
            back = back * r + hat_ref[i, rows - 1 - x]
        sums_ref[pl.ds(i * 2 * depth, depth, stride=2), :] = ahead
        sums_ref[pl.ds(i * 2 * depth + 1, depth, stride=2), :] = back


def ring_kernel(rho_ref, scale_ref, sums_ref, out_ref):
    n_xy = sums_ref.shape[0] // 2
    rho = rho_ref[...]
    ahead = sums_ref[0:1, :]
    back = sums_ref[2 * n_xy - 1 : 2 * n_xy, :]
    for d in range(1, n_xy):
        ahead = ahead * rho + sums_ref[2 * d : 2 * d + 1, :]
        e = n_xy - 1 - d
        back = back * rho + sums_ref[2 * e + 1 : 2 * e + 2, :]
    ahead = ahead * scale_ref[...]
    back = back * scale_ref[...]
    for d in range(n_xy):
        out_ref[2 * d : 2 * d + 1, :] = ahead
        ahead = ahead * rho + sums_ref[2 * d : 2 * d + 1, :]
        e = n_xy - 1 - d
        out_ref[2 * e + 1 : 2 * e + 2, :] = back
        back = back * rho + sums_ref[2 * e + 1 : 2 * e + 2, :]


def solve_kernel(table, decay_ref, hat_ref, enter_ref, out_ref, work_ref, rows_ref):
    n_gz, n_section, n_z, rows, _ = out_ref.shape
    depth = n_gz * n_z
    r = decay_ref[0]
    inverse = decay_ref[1]
    for i in range(n_section):
        value = enter_ref[pl.ds(i * 2 * depth, depth, stride=2), :]
        for x in range(rows):
            source = hat_ref[i, x]
            work_ref[x] = value * r
            value = value * r + source
        value = enter_ref[pl.ds(i * 2 * depth + 1, depth, stride=2), :]
        for x in range(rows - 1, -1, -1):
            value = value * r + hat_ref[i, x]
            rows_ref[i, pl.ds(x, depth, stride=rows), :] = (work_ref[x] + value) * inverse
        planes = [rows_ref[i, pl.ds(k * rows, rows), :] for k in range(depth)]
        for z, plane in enumerate(sine_rows_back(planes, table)):
            out_ref[z // n_z, i, z % n_z] = plane


def sine_rows_back(planes, table):
    depth = len(planes)
    out = [None] * depth
    for z in range(depth // 2):
        parts = []
        for parity in range(2):
            total = planes[parity] * float(table[parity, z])
            for k in range(parity + 2, depth, 2):
                total = total + planes[k] * float(table[k, z])
            parts.append(total)
        out[z] = parts[0] + parts[1]
        out[depth - 1 - z] = parts[0] - parts[1]
    return out


def final_kernel(solved_ref, high_ref, low_ref, out_ref):
    n_gz, n_section, n_z, rows, _ = solved_ref.shape
    modes = jnp.concatenate(
        [solved_ref[g].reshape(n_section * n_z * rows, lanes) for g in range(n_gz)], axis=1
    )
    field = split_dot(modes, high_ref, low_ref)
    out_ref[...] = field.reshape(out_ref.shape)


def on_device(conc_prev, conc_section, potential, diffusivity, charges):
    n_xy = lax.axis_size("xy")
    n_gz = lax.axis_size("gz")
    n_section, n_species, n_z, rows, y_cells = conc_section.shape
    depth = n_z * n_gz
    x_cells = rows * n_xy
    f32 = jnp.float32
    vmem = pl.BlockSpec(memory_space=pltpu.VMEM)
    smem = pl.BlockSpec(memory_space=pltpu.SMEM)
    params = pltpu.CompilerParams(vmem_limit_bytes=40 * 1024 * 1024)
    forward_high, forward_low = cas_halves(y_cells, 1.0 / 32.0)
    sine = sine_matrix(depth)
    decay = jnp.asarray(decay_tables(depth, y_cells, x_cells, rows))

    top = jnp.concatenate([conc_section[:, :, -1], potential[:, None, -1]], axis=1)
    bottom = jnp.concatenate([conc_section[:, :, 0], potential[:, None, 0]], axis=1)
    last = jnp.concatenate([conc_section[:, :, :, -1:], potential[:, None, :, -1:]], axis=1)
    first = jnp.concatenate([conc_section[:, :, :, :1], potential[:, None, :, :1]], axis=1)
    below = lax.ppermute(top, "gz", [(i, i + 1) for i in range(n_gz - 1)])
    above = lax.ppermute(bottom, "gz", [(i + 1, i) for i in range(n_gz - 1)])
    left = lax.ppermute(last, "xy", [(i, (i + 1) % n_xy) for i in range(n_xy)])
    right = lax.ppermute(first, "xy", [((i + 1) % n_xy, i) for i in range(n_xy)])

    butcher = np.asarray(radau_matrix(), np.float32)
    scale_row = 1.0 / (
        1.0 + 6.0 * step_size * np.diag(butcher)[:, None] * diffusivity[None, :]
    )
    coef = (step_size * butcher)[:, :, None] * (diffusivity[None, :] * scale_row)[:, None, :]
    half = 0.5 * charges.astype(f32)
    coef = coef.reshape(-1)

    z_index = lax.axis_index("gz")
    decay_here = lax.dynamic_slice_in_dim(decay, z_index * lanes, lanes, 2)
    kz_here = lax.axis_index("xy") % depth
    rho_here = lax.dynamic_slice_in_dim(decay_here[2], kz_here, 1, 0)
    scale_here = lax.dynamic_slice_in_dim(decay_here[3], kz_here, 1, 0)

    part = pl.pallas_call(
        inner_kernel,
        out_shape=jax.ShapeDtypeStruct(conc_section.shape, f32),
        in_specs=[smem] * 3 + [vmem] * 5,
        out_specs=vmem,
        compiler_params=params,
        cost_estimate=pl.CostEstimate(flops=20_000_000, bytes_accessed=4_500_000, transcendentals=0),
        name="inner_faces",
    )(coef, scale_row.reshape(-1), half, conc_prev, conc_section, potential, left, right)

    conc_new, modes = pl.pallas_call(
        outer_kernel,
        out_shape=(
            jax.ShapeDtypeStruct(conc_section.shape, f32),
            jax.ShapeDtypeStruct((n_gz, n_section, n_z, rows, lanes), f32),
        ),
        in_specs=[smem] * 2 + [vmem] * 7,
        out_specs=(vmem, vmem),
        scratch_shapes=[pltpu.VMEM((n_section, n_z, rows, y_cells), f32)],
        input_output_aliases={2: 0},
        compiler_params=params,
        name="outer_faces",
    )(coef, half, part, conc_section, potential, below, above, forward_high, forward_low)

    columns = lax.all_to_all(modes, "gz", split_axis=0, concat_axis=0, tiled=True)

    n_rows = 2 * n_xy
    hat, sums = pl.pallas_call(
        lambda *refs: sum_kernel(sine, *refs),
        out_shape=(
            jax.ShapeDtypeStruct((n_section, rows, depth, lanes), f32),
            jax.ShapeDtypeStruct((n_rows, lanes), f32),
        ),
        in_specs=[vmem] * 2,
        out_specs=(vmem, vmem),
        scratch_shapes=[pltpu.VMEM((n_section, depth * rows, lanes), f32)],
        compiler_params=params,
        name="block_sums",
    )(decay_here, columns)

    gathered = lax.all_to_all(sums, "xy", split_axis=0, concat_axis=0, tiled=True)
    entering = pl.pallas_call(
        ring_kernel,
        out_shape=jax.ShapeDtypeStruct((n_rows, lanes), f32),
        in_specs=[vmem] * 3,
        out_specs=vmem,
        compiler_params=params,
        name="ring",
    )(rho_here, scale_here, gathered)
    enter = lax.all_to_all(entering, "xy", split_axis=0, concat_axis=0, tiled=True)

    solved = pl.pallas_call(
        lambda *refs: solve_kernel(sine, *refs),
        out_shape=jax.ShapeDtypeStruct((n_gz, n_section, n_z, rows, lanes), f32),
        in_specs=[vmem] * 3,
        out_specs=vmem,
        scratch_shapes=[
            pltpu.VMEM((rows, depth, lanes), f32),
            pltpu.VMEM((n_section, depth * rows, lanes), f32),
        ],
        compiler_params=params,
        name="solve",
    )(decay_here, hat, enter)
    returned = lax.all_to_all(solved, "gz", split_axis=0, concat_axis=0, tiled=True)

    potential_new = pl.pallas_call(
        final_kernel,
        out_shape=jax.ShapeDtypeStruct(potential.shape, f32),
        in_specs=[vmem] * 3,
        out_specs=vmem,
        compiler_params=params,
        name="back_to_y",
    )(returned, forward_high, forward_low)
    return (conc_new, potential_new)


def solution(mesh):
    in_specs = (
        P(None, "gz", "xy", None),
        P(None, None, "gz", "xy", None),
        P(None, "gz", "xy", None),
        P(),
        P(),
    )
    out_specs = (P(None, None, "gz", "xy", None), P(None, "gz", "xy", None))
    return jax.shard_map(
        on_device, mesh=mesh, in_specs=in_specs, out_specs=out_specs, check_vma=False
    )
```

```python
import functools
import math

import jax
import jax.numpy as jnp
import numpy as np
from jax import lax
from jax.experimental import pallas as pl
from jax.experimental.pallas import tpu as pltpu
from jax.sharding import PartitionSpec as P

step_size = 0.2
screening = 0.005
lanes = 128
ring = 16
group = 4
diagonal = math.sqrt(0.5)


def radau_matrix():
    root = math.sqrt(6.0)
    return [
        [(88.0 - 7.0 * root) / 360.0, (296.0 - 169.0 * root) / 1800.0, (-2.0 + 3.0 * root) / 225.0],
        [(296.0 + 169.0 * root) / 1800.0, (88.0 + 7.0 * root) / 360.0, (-2.0 - 3.0 * root) / 225.0],
        [(16.0 - root) / 36.0, (16.0 + root) / 36.0, 1.0 / 9.0],
    ]


def hartley_tables(length):
    b = np.arange(lanes)
    k1 = np.arange(length // lanes)[:, None, None]
    angle = b[:, None] * (k1 + length // lanes * b[None, :]) % length * (2.0 * math.pi / length)
    cas, dif = np.cos(angle) + np.sin(angle), np.sin(angle) - np.cos(angle)
    zero = np.zeros((lanes, lanes))
    pairs = [np.block([[cas[0], zero], [zero, cas[4]]])]
    pairs += [np.block([[cas[p], cas[8 - p]], [dif[p], -dif[8 - p]]]) for p in (1, 2, 3)]
    table = (np.stack(pairs) / math.sqrt(length)).astype(np.float32)
    high = table.astype(jnp.bfloat16)
    low = (table - high.astype(np.float32)).astype(jnp.bfloat16)
    return np.stack([high, low])


def sine_matrix(depth):
    k = np.arange(1, depth + 1)
    return math.sqrt(2.0 / (depth + 1)) * np.sin(np.outer(k, k) * math.pi / (depth + 1))


def decay_tables(depth, y_cells, x_cells, block):
    k1 = y_cells // lanes
    ky = np.arange(k1)[:, None] + k1 * np.arange(lanes)[None, :]
    ez = 2.0 - 2.0 * np.cos(np.arange(1, depth + 1) * math.pi / (depth + 1))
    ey = 2.0 - 2.0 * np.cos(ky.reshape(-1) * 2.0 * math.pi / y_cells)
    lam = screening + ez[:, None] + ey[None, :]
    root = np.sqrt(lam + 0.25 * lam * lam)
    r = 1.0 / (1.0 + 0.5 * lam + root)
    return np.stack([r, 0.5 / root, r**block, 1.0 / (1.0 - r**x_cells)]).astype(np.float32)


def face(near, far, gain):
    return (far - near) + gain * (near + far)


def split_dot(rows, table_ref, pair, contract):
    count = rows.shape[0]
    high = rows.astype(jnp.bfloat16)
    low = (rows - high.astype(jnp.float32)).astype(jnp.bfloat16)

    def product(a, b):
        dims = (((1,), (contract,)), ((), ()))
        return lax.dot_general(a, b, dims, preferred_element_type=jnp.float32)

    main = product(jnp.concatenate([low, high], axis=0), table_ref[0, pair])
    return (product(high, table_ref[1, pair]) + main[:count]) + main[count:]


def halves(value):
    return value[:, :lanes], value[:, lanes:]


def to_modes(rhs, table_ref):
    f = [rhs[:, a * lanes : (a + 1) * lanes] for a in range(8)]
    s = [f[a] + f[a + 4] for a in range(4)]
    d = [f[a] - f[a + 4] for a in range(4)]
    u = diagonal * (d[1] - d[3])
    v = diagonal * (d[1] + d[3])
    even, odd = s[0] + s[2], s[1] + s[3]
    inputs = [
        (even + odd, even - odd),
        (d[0] + u, -(d[2] + v)),
        (s[0] - s[2], s[3] - s[1]),
        (d[0] - u, d[2] - v),
    ]
    blocks = [None] * 8
    for pair, columns in enumerate(inputs):
        out = split_dot(jnp.concatenate(columns, axis=1), table_ref, pair, 0)
        blocks[pair], blocks[8 - pair if pair else 4] = halves(out)
    return blocks


def from_modes(blocks, table_ref):
    outs = []
    for pair in range(4):
        columns = jnp.concatenate([blocks[pair], blocks[8 - pair if pair else 4]], axis=1)
        outs.append(halves(split_dot(columns, table_ref, pair, 1)))
    (p0, p4), (c1, q1), (c2, q2), (c3, q3) = outs
    even, odd = p0 + p4, p0 - p4
    m = diagonal * (c1 - c3)
    n = diagonal * (q1 + q3)
    both, other = c1 + c3, q1 - q3
    return [
        (even + c2) + both,
        (odd - q2) + (m - n),
        (even - c2) - other,
        (odd + q2) - (m + n),
        (even + c2) - both,
        (odd - q2) - (m - n),
        (even - c2) + other,
        (odd + q2) + (m + n),
    ]


def far_layer(n_z):
    return lax.axis_index("gz") % 2 * (n_z - 1)


def far_row(rows):
    return lax.axis_index("xy") % 2 * (rows - 1)


def pack_kernel(
    conc_hbm, pot_hbm, z_far_ref, z_near_ref, x_near_ref, x_far_ref, sems
):
    n_section, n_species, depth, rows, _ = conc_hbm.shape
    z_far = far_layer(depth)
    x_far = far_row(rows)
    copies = []
    for q, (z, ref) in enumerate(((z_far, z_far_ref), (depth - 1 - z_far, z_near_ref))):
        for j in range(n_section):
            pair = [
                pltpu.make_async_copy(
                    conc_hbm.at[j, :, z], ref.at[j, 0:n_species], sems.at[q, j, 0]
                ),
                pltpu.make_async_copy(pot_hbm.at[j, z], ref.at[j, n_species], sems.at[q, j, 1]),
            ]
            for copy in pair:
                copy.start()
            copies.extend(pair)
    for copy in copies:
        copy.wait()
    for x, out_ref in ((x_far, x_far_ref), (rows - 1 - x_far, x_near_ref)):
        for j in range(n_section):
            for q, ref in enumerate((z_far_ref, z_near_ref)):
                for s in range(n_species + 1):
                    to = edge_row(n_section, n_species, depth, j, s, q)
                    out_ref[to : to + 1, :] = ref[j, s, pl.ds(x, 1), :]


def edge_row(n_section, n_species, depth, j, s, q):
    if s < n_species:
        return (j * n_species + s) * depth + q
    return (n_section * n_species + j) * depth + q


def inner_kernel(
    coef_ref, inv_ref, half_ref, prev_ref, z_far_ref, z_near_ref, decay_hbm,
    out_ref, decay_ref, own_ref, sem,
):
    n_section, n_species, depth, rows, y_cells = out_ref.shape
    column = pl.ds(pl.multiple_of(lax.axis_index("gz") * lanes, lanes), lanes)
    decay_copy = pltpu.make_async_copy(decay_hbm.at[:, :, column], decay_ref, sem)
    decay_copy.start()
    row = lax.broadcasted_iota(jnp.int32, (rows, y_cells), 0)
    layers = (z_far_ref, z_near_ref)
    z_far = far_layer(depth)

    def species(s, carry):
        half = half_ref[s]
        totals = []
        for j in range(n_section):
            planes = []
            for ref in layers:
                c = ref[j, s]
                p = ref[j, n_species]
                low = face(pltpu.roll(c, 1, 0), c, half * (p - pltpu.roll(p, 1, 0)))
                low = jnp.where(row == 0, 0.0, low)
                c_next = pltpu.roll(c, y_cells - 1, 1)
                p_next = pltpu.roll(p, y_cells - 1, 1)
                ahead = face(c, c_next, half * (p_next - p))
                planes.append(
                    (pltpu.roll(low, rows - 1, 0) - low) + (ahead - pltpu.roll(ahead, 1, 1))
                )
            step = half * (z_near_ref[j, n_species] - z_far_ref[j, n_species])
            between = face(z_far_ref[j, s], z_near_ref[j, s], step)
            totals.append((planes[0] + between, planes[1] - between))
        for q, z in enumerate((z_far, depth - 1 - z_far)):
            prev = prev_ref[s, z]
            for i in range(n_section):
                c = layers[q][i, s]
                update = inv_ref[i * n_species + s] * (prev - c)
                for j in range(n_section):
                    update = update + coef_ref[(i * n_section + j) * n_species + s] * totals[j][q]
                out_ref[i, s, q] = c + update
        return carry

    lax.fori_loop(0, n_species, species, 0)
    decay_copy.wait()
    index = lax.axis_index("xy")
    solver = index // ring * group + index % group
    own_ref[0:1, :] = decay_ref[2, pl.ds(solver, 1), :]
    own_ref[1:2, :] = decay_ref[3, pl.ds(solver, 1), :]


def outer_kernel(
    coef_ref, half_ref, part_ref, z_far_ref, z_near_ref, z_far_got, z_near_got,
    x_near_sent, x_near_got, x_far_sent, x_far_got, table_ref,
    out_hbm, modes_ref, out_ref, rhs_ref, edge_ref, sems,
):
    n_section, n_species, depth, rows, y_cells = part_ref.shape
    planes = n_species * depth
    kind = lax.broadcasted_iota(jnp.int32, (planes, y_cells), 0) // depth

    def by_species(ref, base):
        value = jnp.full((planes, y_cells), ref[base], jnp.float32)
        for s in range(1, n_species):
            value = jnp.where(kind == s, ref[base + s], value)
        return value

    half_rows = by_species(half_ref, 0)
    sides = ((x_near_sent, x_near_got), (x_far_sent, x_far_got))
    for side, (near, far) in enumerate(sides):
        faces = []
        for j in range(n_section):
            base = n_section * planes + j * depth
            step = far[base : base + depth, :] - near[base : base + depth, :]
            step = jnp.concatenate([step] * n_species, axis=0)
            at = slice(j * planes, (j + 1) * planes)
            faces.append(face(near[at, :], far[at, :], half_rows * step))
        for i in range(n_section):
            update = by_species(coef_ref, i * n_section * n_species) * faces[0]
            for j in range(1, n_section):
                update = update + by_species(coef_ref, (i * n_section + j) * n_species) * faces[j]
            edge_ref[side, i * planes : (i + 1) * planes, :] = update

    pairs = ((z_far_ref, z_far_got), (z_near_ref, z_near_got))
    for i in range(n_section):
        for q in range(depth):
            rhs_ref[i, q] = screening * pairs[q][0][i, n_species]
    row = lax.broadcasted_iota(jnp.int32, (rows, y_cells), 0)
    z_far = far_layer(depth)
    x_far = far_row(rows)
    at_x = (row == rows - 1 - x_far, row == x_far)

    def store(s, q):
        z = z_far if q == 0 else depth - 1 - z_far
        return pltpu.make_async_copy(out_ref.at[:, s, q], out_hbm.at[:, s, z], sems.at[s, q])

    def species(s, carry):
        half = half_ref[s]
        for q, (own, got) in enumerate(pairs):
            faces = []
            for j in range(n_section):
                step = got[j, n_species] - own[j, n_species]
                faces.append(face(own[j, s], got[j, s], half * step))
            for i in range(n_section):
                at = pl.ds(i * planes + s * depth + q, 1)
                update = part_ref[i, s, q]
                for side in range(2):
                    update = update + jnp.where(at_x[side], edge_ref[side, at, :], 0.0)
                for j in range(n_section):
                    update = update + coef_ref[(i * n_section + j) * n_species + s] * faces[j]
                out_ref[i, s, q] = update
                rhs_ref[i, q] += (2.0 * half) * update
            store(s, q).start()
        return carry

    lax.fori_loop(0, n_species, species, 0)
    rhs = rhs_ref[...].reshape(n_section * depth * rows, y_cells)
    for g, block in enumerate(to_modes(rhs, table_ref)):
        modes_ref[g] = block
    for s in range(n_species):
        for q in range(depth):
            store(s, q).wait()


def layer_of(z, n_z):
    g = z // n_z
    return g, int(z % n_z != g % 2 * (n_z - 1))


def sine_rows(planes, table):
    depth = len(planes)
    half = depth // 2
    even = [planes[z] + planes[depth - 1 - z] for z in range(half)]
    odd = [planes[z] - planes[depth - 1 - z] for z in range(half)]
    out = []
    for k in range(depth):
        source = even if k % 2 == 0 else odd
        total = source[0] * float(table[k, 0])
        for z in range(1, half):
            total = total + source[z] * float(table[k, z])
        out.append(total)
    return out


def sine_rows_back(planes, table):
    depth = len(planes)
    out = [None] * depth
    for z in range(depth // 2):
        parts = []
        for parity in range(2):
            total = planes[parity] * float(table[parity, z])
            for k in range(parity + 2, depth, 2):
                total = total + planes[k] * float(table[k, z])
            parts.append(total)
        out[z] = parts[0] + parts[1]
        out[depth - 1 - z] = parts[0] - parts[1]
    return out


def sum_kernel(table, decay_ref, modes_ref, hat_ref, sums_ref, rows_ref):
    n_gz, n_section, n_z, rows, _ = modes_ref.shape
    depth = n_gz * n_z
    r = decay_ref[0]
    where = [layer_of(z, n_z) for z in range(depth)]
    for i in range(n_section):
        planes = [modes_ref[g, i, q] for g, q in where]
        for k, plane in enumerate(sine_rows(planes, table)):
            rows_ref[i, pl.ds(k * rows, rows), :] = plane
        for x in range(rows):
            hat_ref[i, x] = rows_ref[i, pl.ds(x, depth, stride=rows), :]
        ahead = hat_ref[i, 0]
        back = hat_ref[i, rows - 1]
        for x in range(1, rows):
            ahead = ahead * r + hat_ref[i, x]
            back = back * r + hat_ref[i, rows - 1 - x]
        for side, value in enumerate((ahead, back)):
            at = side * n_section + i
            for y in range(depth // group):
                four = value[y * group : (y + 1) * group]
                for copy in range(ring // group):
                    first = (y * ring + copy * group) * 2 * n_section + at
                    sums_ref[pl.ds(first, group, stride=2 * n_section), :] = four


def ring_kernel(n_section, own_ref, sums_ref, out_ref, all_ref):
    per = 2 * n_section
    n_xy = sums_ref.shape[0] // per
    rho = jnp.broadcast_to(own_ref[0:1, :], (n_section, lanes))
    scale = own_ref[1:2, :]

    def ahead_sum(d):
        return sums_ref[d * per : d * per + n_section, :]

    def back_sum(d):
        return sums_ref[d * per + n_section : (d + 1) * per, :]

    ahead = ahead_sum(0)
    back = back_sum(n_xy - 1)
    for d in range(1, n_xy):
        ahead = ahead * rho + ahead_sum(d)
        back = back * rho + back_sum(n_xy - 1 - d)
    ahead = ahead * scale
    back = back * scale
    for d in range(n_xy):
        e = n_xy - 1 - d
        all_ref[d * per : d * per + n_section, :] = ahead
        all_ref[e * per + n_section : (e + 1) * per, :] = back
        ahead = ahead * rho + ahead_sum(d)
        back = back * rho + back_sum(e)
    mine = lax.axis_index("xy") % ring // group
    span = group * per
    for y in range(n_xy // ring):
        first = pl.multiple_of(y * ring * per + mine * span, 8)
        out_ref[y * span : (y + 1) * span, :] = all_ref[pl.ds(first, span), :]


def solve_kernel(table, decay_ref, hat_ref, enter_ref, out_ref, work_ref, rows_ref):
    n_gz, n_section, n_z, rows, _ = out_ref.shape
    depth = n_gz * n_z
    r = decay_ref[0]
    inverse = decay_ref[1]
    where = [layer_of(z, n_z) for z in range(depth)]
    for i in range(n_section):
        value = enter_ref[pl.ds(i, depth, stride=2 * n_section), :]
        for x in range(rows):
            source = hat_ref[i, x]
            work_ref[x] = value * r
            value = value * r + source
        value = enter_ref[pl.ds(n_section + i, depth, stride=2 * n_section), :]
        for x in range(rows - 1, -1, -1):
            value = value * r + hat_ref[i, x]
            rows_ref[i, pl.ds(x, depth, stride=rows), :] = (work_ref[x] + value) * inverse
        planes = [rows_ref[i, pl.ds(k * rows, rows), :] for k in range(depth)]
        for (g, q), plane in zip(where, sine_rows_back(planes, table)):
            out_ref[g, i, q] = plane


def final_kernel(solved_ref, table_ref, out_ref):
    n_gz, n_section, n_z, rows, _ = solved_ref.shape
    z_far = far_layer(n_z)
    blocks = [solved_ref[g].reshape(n_section * n_z * rows, lanes) for g in range(n_gz)]
    for a, block in enumerate(from_modes(blocks, table_ref)):
        block = block.reshape(n_section, n_z, rows, lanes)
        for i in range(n_section):
            for q, z in enumerate((z_far, n_z - 1 - z_far)):
                out_ref[i, z, :, a * lanes : (a + 1) * lanes] = block[i, q]


def on_device(conc_prev, conc_section, potential, diffusivity, charges):
    n_xy = lax.axis_size("xy")
    n_gz = lax.axis_size("gz")
    n_section, n_species, n_z, rows, y_cells = conc_section.shape
    depth = n_z * n_gz
    x_cells = rows * n_xy
    f32 = jnp.float32
    vmem = pl.BlockSpec(memory_space=pltpu.VMEM)
    smem = pl.BlockSpec(memory_space=pltpu.SMEM)
    hbm = pl.BlockSpec(memory_space=pltpu.HBM)

    def params(mib):
        return pltpu.CompilerParams(vmem_limit_bytes=mib * 1024 * 1024)

    table = jnp.asarray(hartley_tables(y_cells))
    sine = sine_matrix(depth)
    decay = jnp.asarray(decay_tables(depth, y_cells, x_cells, rows))

    layers = jax.ShapeDtypeStruct((n_section, n_species + 1, rows, y_cells), f32)
    edges = jax.ShapeDtypeStruct((n_section * n_z * (n_species + 1), y_cells), f32)
    z_far_out, z_near_out, x_near_out, x_far_out = pl.pallas_call(
        pack_kernel,
        out_shape=(layers, layers, edges, edges),
        in_specs=[hbm] * 2,
        out_specs=(vmem,) * 4,
        scratch_shapes=[pltpu.SemaphoreType.DMA((n_z, n_section, 2))],
        compiler_params=params(50),
        name="pack",
    )(conc_section, potential)

    def swap(value, axis, pairs):
        return lax.ppermute(value, axis, pairs + [(j, i) for i, j in pairs])

    z_far_in = swap(z_far_out, "gz", [(i, i + 1) for i in range(1, n_gz - 1, 2)])
    z_near_in = swap(z_near_out, "gz", [(i, i + 1) for i in range(0, n_gz, 2)])
    x_near_in = swap(x_near_out, "xy", [(i, i + 1) for i in range(0, n_xy, 2)])
    x_far_in = swap(x_far_out, "xy", [(i, (i + 1) % n_xy) for i in range(1, n_xy, 2)])

    butcher = np.asarray(radau_matrix(), np.float32)
    scale_row = 1.0 / (
        1.0 + 6.0 * step_size * np.diag(butcher)[:, None] * diffusivity[None, :]
    )
    coef = (step_size * butcher)[:, :, None] * (diffusivity[None, :] * scale_row)[:, None, :]
    half = 0.5 * charges.astype(f32)
    coef = coef.reshape(-1)

    planes = (n_section, n_species, n_z, rows, y_cells)
    part, decay_here, own = pl.pallas_call(
        inner_kernel,
        out_shape=(
            jax.ShapeDtypeStruct(planes, f32),
            jax.ShapeDtypeStruct((decay.shape[0], depth, lanes), f32),
            jax.ShapeDtypeStruct((2, lanes), f32),
        ),
        in_specs=[smem] * 3 + [vmem] * 3 + [hbm],
        out_specs=(vmem, vmem, vmem),
        scratch_shapes=[pltpu.SemaphoreType.DMA(())],
        compiler_params=params(24),
        cost_estimate=pl.CostEstimate(flops=20_000_000, bytes_accessed=4_500_000, transcendentals=0),
        name="inner_faces",
    )(coef, scale_row.reshape(-1), half, conc_prev, z_far_out, z_near_out, decay)

    conc_new, modes = pl.pallas_call(
        outer_kernel,
        out_shape=(
            jax.ShapeDtypeStruct(conc_section.shape, f32),
            jax.ShapeDtypeStruct((n_gz, n_section * n_z * rows, lanes), f32),
        ),
        in_specs=[smem] * 2 + [vmem] * 10,
        out_specs=(hbm, vmem),
        scratch_shapes=[
            pltpu.VMEM(planes, f32),
            pltpu.VMEM((n_section, n_z, rows, y_cells), f32),
            pltpu.VMEM((2, n_section * n_species * n_z, y_cells), f32),
            pltpu.SemaphoreType.DMA((n_species, n_z)),
        ],
        compiler_params=params(24),
        name="outer_faces",
    )(
        coef, half, part, z_far_out, z_near_out, z_far_in, z_near_in,
        x_near_out, x_near_in, x_far_out, x_far_in, table,
    )

    columns = lax.all_to_all(modes, "gz", split_axis=0, concat_axis=0, tiled=True)
    columns = columns.reshape(n_gz, n_section, n_z, rows, lanes)

    n_rows = 2 * n_section * n_xy
    hat, sums = pl.pallas_call(
        functools.partial(sum_kernel, sine),
        out_shape=(
            jax.ShapeDtypeStruct((n_section, rows, depth, lanes), f32),
            jax.ShapeDtypeStruct((n_rows, lanes), f32),
        ),
        in_specs=[vmem] * 2,
        out_specs=(vmem, vmem),
        scratch_shapes=[pltpu.VMEM((n_section, depth * rows, lanes), f32)],
        compiler_params=params(12),
        name="block_sums",
    )(decay_here, columns)

    sums = sums.reshape(n_xy, n_section, 2, lanes)
    gathered = lax.all_to_all(sums, "xy", split_axis=0, concat_axis=0, tiled=True)
    gathered = gathered.reshape(n_rows, lanes)
    entering = pl.pallas_call(
        functools.partial(ring_kernel, n_section),
        out_shape=jax.ShapeDtypeStruct((2 * n_section * depth, lanes), f32),
        in_specs=[vmem] * 2,
        out_specs=vmem,
        scratch_shapes=[pltpu.VMEM((n_rows, lanes), f32)],
        compiler_params=params(12),
        name="ring",
    )(own, gathered)
    sharers = [
        [y * ring + first + z for y in range(n_xy // ring) for z in range(group)]
        for first in range(0, ring, group)
    ]
    entering = entering.reshape(depth, n_section, 2, lanes)
    enter = lax.all_to_all(
        entering, "xy", split_axis=0, concat_axis=0, tiled=True, axis_index_groups=sharers
    )
    enter = enter.reshape(2 * n_section * depth, lanes)

    solved = pl.pallas_call(
        functools.partial(solve_kernel, sine),
        out_shape=jax.ShapeDtypeStruct((n_gz, n_section, n_z, rows, lanes), f32),
        in_specs=[vmem] * 3,
        out_specs=vmem,
        scratch_shapes=[
            pltpu.VMEM((rows, depth, lanes), f32),
            pltpu.VMEM((n_section, depth * rows, lanes), f32),
        ],
        compiler_params=params(12),
        name="solve",
    )(decay_here, hat, enter)
    returned = lax.all_to_all(solved, "gz", split_axis=0, concat_axis=0, tiled=True)

    potential_new = pl.pallas_call(
        final_kernel,
        out_shape=jax.ShapeDtypeStruct(potential.shape, f32),
        in_specs=[vmem] * 2,
        out_specs=vmem,
        compiler_params=params(12),
        name="back_to_y",
    )(returned, table)
    return (conc_new, potential_new)


def solution(mesh):
    in_specs = (
        P(None, "gz", "xy", None),
        P(None, None, "gz", "xy", None),
        P(None, "gz", "xy", None),
        P(),
        P(),
    )
    out_specs = (P(None, None, "gz", "xy", None), P(None, "gz", "xy", None))
    return jax.shard_map(
        on_device, mesh=mesh, in_specs=in_specs, out_specs=out_specs, check_vma=False
    )
```

```python
import functools
import math

import jax
import jax.numpy as jnp
import numpy as np
from jax import lax
from jax.experimental import pallas as pl
from jax.experimental.pallas import tpu as pltpu
from jax.sharding import PartitionSpec as P

step_size = 0.2
screening = 0.005
lanes = 128
ring = 16
group = 4
diagonal = math.sqrt(0.5)


def radau_matrix():
    root = math.sqrt(6.0)
    return [
        [(88.0 - 7.0 * root) / 360.0, (296.0 - 169.0 * root) / 1800.0, (-2.0 + 3.0 * root) / 225.0],
        [(296.0 + 169.0 * root) / 1800.0, (88.0 + 7.0 * root) / 360.0, (-2.0 - 3.0 * root) / 225.0],
        [(16.0 - root) / 36.0, (16.0 + root) / 36.0, 1.0 / 9.0],
    ]


def hartley_tables(length):
    b = np.arange(lanes)
    k1 = np.arange(length // lanes)[:, None, None]
    angle = b[:, None] * (k1 + length // lanes * b[None, :]) % length * (2.0 * math.pi / length)
    cas, dif = np.cos(angle) + np.sin(angle), np.sin(angle) - np.cos(angle)
    zero = np.zeros((lanes, lanes))
    pairs = [np.block([[cas[0], zero], [zero, cas[4]]])]
    pairs += [np.block([[cas[p], cas[8 - p]], [dif[p], -dif[8 - p]]]) for p in (1, 2, 3)]
    table = (np.stack(pairs) / math.sqrt(length)).astype(np.float32)
    high = table.astype(jnp.bfloat16)
    low = (table - high.astype(np.float32)).astype(jnp.bfloat16)
    return np.stack([high, low])


def sine_matrix(depth):
    k = np.arange(1, depth + 1)
    return math.sqrt(2.0 / (depth + 1)) * np.sin(np.outer(k, k) * math.pi / (depth + 1))


def wave_table(depth, y_cells):
    k1 = y_cells // lanes
    ky = np.arange(k1)[:, None] + k1 * np.arange(lanes)[None, :]
    ey = 2.0 - 2.0 * np.cos(ky * 2.0 * math.pi / y_cells)
    ez = 2.0 - 2.0 * np.cos(np.arange(1, depth + 1) * math.pi / (depth + 1))
    return np.concatenate([ey, np.broadcast_to(ez[:, None], (depth, lanes))]).astype(np.float32)


def power(value, exponent):
    for _ in range(exponent.bit_length() - 1):
        value = value * value
    return value


def face(near, far, gain):
    return (far - near) + gain * (near + far)


def split_dot(rows, table_ref, pair, contract):
    count = rows.shape[0]
    high = rows.astype(jnp.bfloat16)
    low = (rows - high.astype(jnp.float32)).astype(jnp.bfloat16)

    def product(a, b):
        dims = (((1,), (contract,)), ((), ()))
        return lax.dot_general(a, b, dims, preferred_element_type=jnp.float32)

    main = product(jnp.concatenate([low, high], axis=0), table_ref[0, pair])
    return (product(high, table_ref[1, pair]) + main[:count]) + main[count:]


def halves(value):
    return value[:, :lanes], value[:, lanes:]


def to_modes(rhs, table_ref):
    f = [rhs[:, a * lanes : (a + 1) * lanes] for a in range(8)]
    s = [f[a] + f[a + 4] for a in range(4)]
    d = [f[a] - f[a + 4] for a in range(4)]
    u = diagonal * (d[1] - d[3])
    v = diagonal * (d[1] + d[3])
    even, odd = s[0] + s[2], s[1] + s[3]
    inputs = [
        (even + odd, even - odd),
        (d[0] + u, -(d[2] + v)),
        (s[0] - s[2], s[3] - s[1]),
        (d[0] - u, d[2] - v),
    ]
    blocks = [None] * 8
    for pair, columns in enumerate(inputs):
        out = split_dot(jnp.concatenate(columns, axis=1), table_ref, pair, 0)
        blocks[pair], blocks[8 - pair if pair else 4] = halves(out)
    return blocks


def from_modes(blocks, table_ref):
    outs = []
    for pair in range(4):
        columns = jnp.concatenate([blocks[pair], blocks[8 - pair if pair else 4]], axis=1)
        outs.append(halves(split_dot(columns, table_ref, pair, 1)))
    (p0, p4), (c1, q1), (c2, q2), (c3, q3) = outs
    even, odd = p0 + p4, p0 - p4
    m = diagonal * (c1 - c3)
    n = diagonal * (q1 + q3)
    both, other = c1 + c3, q1 - q3
    return [
        (even + c2) + both,
        (odd - q2) + (m - n),
        (even - c2) - other,
        (odd + q2) - (m + n),
        (even + c2) - both,
        (odd - q2) - (m - n),
        (even - c2) + other,
        (odd + q2) + (m + n),
    ]


def coefficients(diffusivity_ref, s):
    matrix = radau_matrix()
    d = diffusivity_ref[s]
    inverse, coef = [], []
    for i, row in enumerate(matrix):
        inverse.append(1.0 / (1.0 + (6.0 * step_size * row[i]) * d))
        coef.append([(step_size * entry) * d * inverse[i] for entry in row])
    return inverse, coef


def far_layer(n_z):
    return lax.axis_index("gz") % 2 * (n_z - 1)


def far_row(rows):
    return lax.axis_index("xy") % 2 * (rows - 1)


def pack_kernel(
    conc_hbm, pot_hbm, z_far_ref, z_near_ref, x_near_ref, x_far_ref, sems
):
    n_section, n_species, depth, rows, _ = conc_hbm.shape
    z_far = far_layer(depth)
    x_far = far_row(rows)
    copies = []
    for q, (z, ref) in enumerate(((z_far, z_far_ref), (depth - 1 - z_far, z_near_ref))):
        for j in range(n_section):
            pair = [
                pltpu.make_async_copy(
                    conc_hbm.at[j, :, z], ref.at[j, 0:n_species], sems.at[q, j, 0]
                ),
                pltpu.make_async_copy(pot_hbm.at[j, z], ref.at[j, n_species], sems.at[q, j, 1]),
            ]
            for copy in pair:
                copy.start()
            copies.extend(pair)
    for copy in copies:
        copy.wait()
    for x, out_ref in ((x_far, x_far_ref), (rows - 1 - x_far, x_near_ref)):
        for j in range(n_section):
            for q, ref in enumerate((z_far_ref, z_near_ref)):
                for s in range(n_species + 1):
                    to = edge_row(n_section, n_species, depth, j, s, q)
                    out_ref[to : to + 1, :] = ref[j, s, pl.ds(x, 1), :]


def edge_row(n_section, n_species, depth, j, s, q):
    if s < n_species:
        return (j * n_species + s) * depth + q
    return (n_section * n_species + j) * depth + q


def inner_kernel(
    diffusivity_ref, charge_ref, prev_ref, z_far_ref, z_near_ref, wave_ref,
    out_ref, decay_ref, own_ref, step_ref, between_ref,
):
    n_section, n_species, depth, rows, y_cells = out_ref.shape
    row = lax.broadcasted_iota(jnp.int32, (rows, y_cells), 0)
    layers = (z_far_ref, z_near_ref)
    z_far = far_layer(depth)
    for j in range(n_section):
        for q, ref in enumerate(layers):
            p = ref[j, n_species]
            step_ref[j, q, 0] = p - pltpu.roll(p, 1, 0)
            step_ref[j, q, 1] = pltpu.roll(p, y_cells - 1, 1) - p
        between_ref[j] = z_near_ref[j, n_species] - z_far_ref[j, n_species]

    def species(s, carry):
        half = 0.5 * charge_ref[s].astype(jnp.float32)
        inverse, coef = coefficients(diffusivity_ref, s)
        totals = []
        for j in range(n_section):
            planes = []
            for q, ref in enumerate(layers):
                c = ref[j, s]
                low = face(pltpu.roll(c, 1, 0), c, half * step_ref[j, q, 0])
                low = jnp.where(row == 0, 0.0, low)
                ahead = face(c, pltpu.roll(c, y_cells - 1, 1), half * step_ref[j, q, 1])
                planes.append(
                    (pltpu.roll(low, rows - 1, 0) - low) + (ahead - pltpu.roll(ahead, 1, 1))
                )
            between = face(z_far_ref[j, s], z_near_ref[j, s], half * between_ref[j])
            totals.append((planes[0] + between, planes[1] - between))
        for q, z in enumerate((z_far, depth - 1 - z_far)):
            prev = prev_ref[s, z]
            for i in range(n_section):
                c = layers[q][i, s]
                update = inverse[i] * (prev - c)
                for j in range(n_section):
                    update = update + coef[i][j] * totals[j][q]
                out_ref[i, s, q] = c + update
        return carry

    lax.fori_loop(0, n_species, species, 0)
    k1 = wave_ref.shape[0] - decay_ref.shape[1]
    lam = screening + wave_ref[pl.ds(lax.axis_index("gz"), 1), :] + wave_ref[k1:, :]
    root = jnp.sqrt(lam + 0.25 * lam * lam)
    r = 1.0 / (1.0 + 0.5 * lam + root)
    decay_ref[0] = r
    decay_ref[1] = 0.5 / root
    decay_ref[2] = power(r, rows)
    index = lax.axis_index("xy")
    solver = index // ring * group + index % group
    rho = decay_ref[2, pl.ds(solver, 1), :]
    own_ref[0:1, :] = rho
    own_ref[1:2, :] = 1.0 / (1.0 - power(rho, lax.axis_size("xy")))


def outer_kernel(
    diffusivity_ref, charge_ref, part_ref, z_far_ref, z_near_ref, z_far_got,
    x_far_sent, x_far_got, x_near_sent, x_near_got, z_near_got, table_ref,
    out_hbm, modes_ref, out_ref, rhs_ref, edge_ref, sems,
):
    n_section, n_species, depth, rows, y_cells = part_ref.shape
    planes = n_species * depth
    kind = lax.broadcasted_iota(jnp.int32, (planes, y_cells), 0) // depth
    by_row = [coefficients(diffusivity_ref, s)[1] for s in range(n_species)]

    def by_species(values):
        total = jnp.full((planes, y_cells), values[0], jnp.float32)
        for s in range(1, n_species):
            total = jnp.where(kind == s, values[s], total)
        return total

    half_rows = by_species([0.5 * charge_ref[s].astype(jnp.float32) for s in range(n_species)])
    sides = ((x_near_sent, x_near_got), (x_far_sent, x_far_got))
    faces = []
    for near, far in sides:
        for j in range(n_section):
            base = n_section * planes + j * depth
            step = far[base : base + depth, :] - near[base : base + depth, :]
            step = jnp.concatenate([step] * n_species, axis=0)
            at = slice(j * planes, (j + 1) * planes)
            faces.append(face(near[at, :], far[at, :], half_rows * step))
    for i in range(n_section):
        weights = [by_species([by_row[s][i][j] for s in range(n_species)]) for j in range(n_section)]
        for side in range(2):
            update = weights[0] * faces[side * n_section]
            for j in range(1, n_section):
                update = update + weights[j] * faces[side * n_section + j]
            edge_ref[side, i * planes : (i + 1) * planes, :] = update

    pairs = ((z_far_ref, z_far_got), (z_near_ref, z_near_got))
    for i in range(n_section):
        for q in range(depth):
            rhs_ref[i, q] = screening * pairs[q][0][i, n_species]
    row = lax.broadcasted_iota(jnp.int32, (rows, y_cells), 0)
    z_far = far_layer(depth)
    x_far = far_row(rows)
    at_x = (row == rows - 1 - x_far, row == x_far)

    def store(s, q):
        z = z_far if q == 0 else depth - 1 - z_far
        return pltpu.make_async_copy(out_ref.at[:, s, q], out_hbm.at[:, s, z], sems.at[s, q])

    def species(s, carry):
        half = 0.5 * charge_ref[s].astype(jnp.float32)
        _, coef = coefficients(diffusivity_ref, s)
        for q, (own, got) in enumerate(pairs):
            faces = []
            for j in range(n_section):
                step = got[j, n_species] - own[j, n_species]
                faces.append(face(own[j, s], got[j, s], half * step))
            for i in range(n_section):
                at = pl.ds(i * planes + s * depth + q, 1)
                update = part_ref[i, s, q]
                for side in range(2):
                    update = update + jnp.where(at_x[side], edge_ref[side, at, :], 0.0)
                for j in range(n_section):
                    update = update + coef[i][j] * faces[j]
                out_ref[i, s, q] = update
                rhs_ref[i, q] += (2.0 * half) * update
            store(s, q).start()
        return carry

    lax.fori_loop(0, n_species, species, 0)
    rhs = rhs_ref[...].reshape(n_section * depth * rows, y_cells)
    for g, block in enumerate(to_modes(rhs, table_ref)):
        modes_ref[g] = block
    for s in range(n_species):
        for q in range(depth):
            store(s, q).wait()


def layer_of(z, n_z):
    g = z // n_z
    return g, int(z % n_z != g % 2 * (n_z - 1))


def sine_rows(planes, table):
    depth = len(planes)
    half = depth // 2
    even = [planes[z] + planes[depth - 1 - z] for z in range(half)]
    odd = [planes[z] - planes[depth - 1 - z] for z in range(half)]
    out = []
    for k in range(depth):
        source = even if k % 2 == 0 else odd
        total = source[0] * float(table[k, 0])
        for z in range(1, half):
            total = total + source[z] * float(table[k, z])
        out.append(total)
    return out


def sine_rows_back(planes, table):
    depth = len(planes)
    out = [None] * depth
    for z in range(depth // 2):
        parts = []
        for parity in range(2):
            total = planes[parity] * float(table[parity, z])
            for k in range(parity + 2, depth, 2):
                total = total + planes[k] * float(table[k, z])
            parts.append(total)
        out[z] = parts[0] + parts[1]
        out[depth - 1 - z] = parts[0] - parts[1]
    return out


def sum_kernel(table, decay_ref, modes_ref, hat_ref, sums_ref, rows_ref):
    n_gz, n_section, n_z, rows, _ = modes_ref.shape
    depth = n_gz * n_z
    r = decay_ref[0]
    where = [layer_of(z, n_z) for z in range(depth)]
    for i in range(n_section):
        planes = [modes_ref[g, i, q] for g, q in where]
        for k, plane in enumerate(sine_rows(planes, table)):
            rows_ref[i, pl.ds(k * rows, rows), :] = plane
        for x in range(rows):
            hat_ref[i, x] = rows_ref[i, pl.ds(x, depth, stride=rows), :]
        ahead = hat_ref[i, 0]
        back = hat_ref[i, rows - 1]
        for x in range(1, rows):
            ahead = ahead * r + hat_ref[i, x]
            back = back * r + hat_ref[i, rows - 1 - x]
        for side, value in enumerate((ahead, back)):
            at = side * n_section + i
            for y in range(depth // group):
                four = value[y * group : (y + 1) * group]
                for copy in range(ring // group):
                    first = (y * ring + copy * group) * 2 * n_section + at
                    sums_ref[pl.ds(first, group, stride=2 * n_section), :] = four


def ring_kernel(n_section, own_ref, sums_ref, out_ref, all_ref):
    per = 2 * n_section
    n_xy = sums_ref.shape[0] // per
    rho = jnp.broadcast_to(own_ref[0:1, :], (n_section, lanes))
    scale = own_ref[1:2, :]

    def ahead_sum(d):
        return sums_ref[d * per : d * per + n_section, :]

    def back_sum(d):
        return sums_ref[d * per + n_section : (d + 1) * per, :]

    ahead = ahead_sum(0)
    back = back_sum(n_xy - 1)
    for d in range(1, n_xy):
        ahead = ahead * rho + ahead_sum(d)
        back = back * rho + back_sum(n_xy - 1 - d)
    ahead = ahead * scale
    back = back * scale
    for d in range(n_xy):
        e = n_xy - 1 - d
        all_ref[d * per : d * per + n_section, :] = ahead
        all_ref[e * per + n_section : (e + 1) * per, :] = back
        ahead = ahead * rho + ahead_sum(d)
        back = back * rho + back_sum(e)
    mine = lax.axis_index("xy") % ring // group
    span = group * per
    for y in range(n_xy // ring):
        first = pl.multiple_of(y * ring * per + mine * span, 8)
        out_ref[y * span : (y + 1) * span, :] = all_ref[pl.ds(first, span), :]


def solve_kernel(table, decay_ref, hat_ref, enter_ref, out_ref, work_ref, rows_ref):
    n_gz, n_section, n_z, rows, _ = out_ref.shape
    depth = n_gz * n_z
    r = decay_ref[0]
    inverse = decay_ref[1]
    where = [layer_of(z, n_z) for z in range(depth)]
    for i in range(n_section):
        value = enter_ref[pl.ds(i, depth, stride=2 * n_section), :]
        for x in range(rows):
            source = hat_ref[i, x]
            work_ref[x] = value * r
            value = value * r + source
        value = enter_ref[pl.ds(n_section + i, depth, stride=2 * n_section), :]
        for x in range(rows - 1, -1, -1):
            value = value * r + hat_ref[i, x]
            rows_ref[i, pl.ds(x, depth, stride=rows), :] = (work_ref[x] + value) * inverse
        planes = [rows_ref[i, pl.ds(k * rows, rows), :] for k in range(depth)]
        for (g, q), plane in zip(where, sine_rows_back(planes, table)):
            out_ref[g, i, q] = plane


def final_kernel(solved_ref, table_ref, out_ref):
    n_gz, n_section, n_z, rows, _ = solved_ref.shape
    z_far = far_layer(n_z)
    blocks = [solved_ref[g].reshape(n_section * n_z * rows, lanes) for g in range(n_gz)]
    for a, block in enumerate(from_modes(blocks, table_ref)):
        block = block.reshape(n_section, n_z, rows, lanes)
        for i in range(n_section):
            for q, z in enumerate((z_far, n_z - 1 - z_far)):
                out_ref[i, z, :, a * lanes : (a + 1) * lanes] = block[i, q]


def on_device(conc_prev, conc_section, potential, diffusivity, charges):
    n_xy = lax.axis_size("xy")
    n_gz = lax.axis_size("gz")
    n_section, n_species, n_z, rows, y_cells = conc_section.shape
    depth = n_z * n_gz
    f32 = jnp.float32
    vmem = pl.BlockSpec(memory_space=pltpu.VMEM)
    smem = pl.BlockSpec(memory_space=pltpu.SMEM)
    hbm = pl.BlockSpec(memory_space=pltpu.HBM)

    def params(mib):
        return pltpu.CompilerParams(vmem_limit_bytes=mib * 1024 * 1024)

    table = jnp.asarray(hartley_tables(y_cells))
    sine = sine_matrix(depth)
    wave = jnp.asarray(wave_table(depth, y_cells))

    layers = jax.ShapeDtypeStruct((n_section, n_species + 1, rows, y_cells), f32)
    edges = jax.ShapeDtypeStruct((n_section * n_z * (n_species + 1), y_cells), f32)
    z_far_out, z_near_out, x_near_out, x_far_out = pl.pallas_call(
        pack_kernel,
        out_shape=(layers, layers, edges, edges),
        in_specs=[hbm] * 2,
        out_specs=(vmem,) * 4,
        scratch_shapes=[pltpu.SemaphoreType.DMA((n_z, n_section, 2))],
        compiler_params=params(50),
        name="pack",
    )(conc_section, potential)

    def swap(value, axis, pairs):
        return lax.ppermute(value, axis, pairs + [(j, i) for i, j in pairs])

    z_far_in = swap(z_far_out, "gz", [(i, i + 1) for i in range(1, n_gz - 1, 2)])
    x_far_in = swap(x_far_out, "xy", [(i, (i + 1) % n_xy) for i in range(1, n_xy, 2)])
    x_near_in = swap(x_near_out, "xy", [(i, i + 1) for i in range(0, n_xy, 2)])
    z_near_in = swap(z_near_out, "gz", [(i, i + 1) for i in range(0, n_gz, 2)])

    planes = (n_section, n_species, n_z, rows, y_cells)
    part, decay_here, own = pl.pallas_call(
        inner_kernel,
        out_shape=(
            jax.ShapeDtypeStruct(planes, f32),
            jax.ShapeDtypeStruct((3, depth, lanes), f32),
            jax.ShapeDtypeStruct((2, lanes), f32),
        ),
        in_specs=[smem] * 2 + [vmem] * 4,
        out_specs=(vmem, vmem, vmem),
        scratch_shapes=[
            pltpu.VMEM((n_section, n_z, 2, rows, y_cells), f32),
            pltpu.VMEM((n_section, rows, y_cells), f32),
        ],
        compiler_params=params(24),
        cost_estimate=pl.CostEstimate(flops=20_000_000, bytes_accessed=4_500_000, transcendentals=0),
        name="inner_faces",
    )(diffusivity, charges, conc_prev, z_far_out, z_near_out, wave)

    conc_new, modes = pl.pallas_call(
        outer_kernel,
        out_shape=(
            jax.ShapeDtypeStruct(conc_section.shape, f32),
            jax.ShapeDtypeStruct((n_gz, n_section * n_z * rows, lanes), f32),
        ),
        in_specs=[smem] * 2 + [vmem] * 10,
        out_specs=(hbm, vmem),
        scratch_shapes=[
            pltpu.VMEM(planes, f32),
            pltpu.VMEM((n_section, n_z, rows, y_cells), f32),
            pltpu.VMEM((2, n_section * n_species * n_z, y_cells), f32),
            pltpu.SemaphoreType.DMA((n_species, n_z)),
        ],
        compiler_params=params(24),
        name="outer_faces",
    )(
        diffusivity, charges, part, z_far_out, z_near_out, z_far_in,
        x_far_out, x_far_in, x_near_out, x_near_in, z_near_in, table,
    )

    columns = lax.all_to_all(modes, "gz", split_axis=0, concat_axis=0, tiled=True)
    columns = columns.reshape(n_gz, n_section, n_z, rows, lanes)

    n_rows = 2 * n_section * n_xy
    hat, sums = pl.pallas_call(
        functools.partial(sum_kernel, sine),
        out_shape=(
            jax.ShapeDtypeStruct((n_section, rows, depth, lanes), f32),
            jax.ShapeDtypeStruct((n_rows, lanes), f32),
        ),
        in_specs=[vmem] * 2,
        out_specs=(vmem, vmem),
        scratch_shapes=[pltpu.VMEM((n_section, depth * rows, lanes), f32)],
        compiler_params=params(12),
        name="block_sums",
    )(decay_here, columns)

    sums = sums.reshape(n_xy, n_section, 2, lanes)
    gathered = lax.all_to_all(sums, "xy", split_axis=0, concat_axis=0, tiled=True)
    gathered = gathered.reshape(n_rows, lanes)
    entering = pl.pallas_call(
        functools.partial(ring_kernel, n_section),
        out_shape=jax.ShapeDtypeStruct((2 * n_section * depth, lanes), f32),
        in_specs=[vmem] * 2,
        out_specs=vmem,
        scratch_shapes=[pltpu.VMEM((n_rows, lanes), f32)],
        compiler_params=params(12),
        name="ring",
    )(own, gathered)
    sharers = [
        [y * ring + first + z for y in range(n_xy // ring) for z in range(group)]
        for first in range(0, ring, group)
    ]
    entering = entering.reshape(depth, n_section, 2, lanes)
    enter = lax.all_to_all(
        entering, "xy", split_axis=0, concat_axis=0, tiled=True, axis_index_groups=sharers
    )
    enter = enter.reshape(2 * n_section * depth, lanes)

    solved = pl.pallas_call(
        functools.partial(solve_kernel, sine),
        out_shape=jax.ShapeDtypeStruct((n_gz, n_section, n_z, rows, lanes), f32),
        in_specs=[vmem] * 3,
        out_specs=vmem,
        scratch_shapes=[
            pltpu.VMEM((rows, depth, lanes), f32),
            pltpu.VMEM((n_section, depth * rows, lanes), f32),
        ],
        compiler_params=params(12),
        name="solve",
    )(decay_here, hat, enter)
    returned = lax.all_to_all(solved, "gz", split_axis=0, concat_axis=0, tiled=True)

    potential_new = pl.pallas_call(
        final_kernel,
        out_shape=jax.ShapeDtypeStruct(potential.shape, f32),
        in_specs=[vmem] * 2,
        out_specs=vmem,
        compiler_params=params(12),
        name="back_to_y",
    )(returned, table)
    return (conc_new, potential_new)


def solution(mesh):
    in_specs = (
        P(None, "gz", "xy", None),
        P(None, None, "gz", "xy", None),
        P(None, "gz", "xy", None),
        P(),
        P(),
    )
    out_specs = (P(None, None, "gz", "xy", None), P(None, "gz", "xy", None))
    return jax.shard_map(
        on_device, mesh=mesh, in_specs=in_specs, out_specs=out_specs, check_vma=False
    )
```

```python
import functools
import math

import jax
import jax.numpy as jnp
import numpy as np
from jax import lax
from jax.experimental import pallas as pl
from jax.experimental.pallas import tpu as pltpu
from jax.sharding import PartitionSpec as P

step_size = 0.2
screening = 0.005
lanes = 128
ring = 16
group = 4
diagonal = math.sqrt(0.5)


def radau_matrix():
    root = math.sqrt(6.0)
    return [
        [(88.0 - 7.0 * root) / 360.0, (296.0 - 169.0 * root) / 1800.0, (-2.0 + 3.0 * root) / 225.0],
        [(296.0 + 169.0 * root) / 1800.0, (88.0 + 7.0 * root) / 360.0, (-2.0 - 3.0 * root) / 225.0],
        [(16.0 - root) / 36.0, (16.0 + root) / 36.0, 1.0 / 9.0],
    ]


def hartley_tables(length):
    b = np.arange(lanes)
    k1 = np.arange(length // lanes)[:, None, None]
    angle = b[:, None] * (k1 + length // lanes * b[None, :]) % length * (2.0 * math.pi / length)
    cas, dif = np.cos(angle) + np.sin(angle), np.sin(angle) - np.cos(angle)
    zero = np.zeros((lanes, lanes))
    pairs = [np.block([[cas[0], zero], [zero, cas[4]]])]
    pairs += [np.block([[cas[p], cas[8 - p]], [dif[p], -dif[8 - p]]]) for p in (1, 2, 3)]
    table = (np.stack(pairs) / math.sqrt(length)).astype(np.float32)
    high = table.astype(jnp.bfloat16)
    low = (table - high.astype(np.float32)).astype(jnp.bfloat16)
    return np.stack([high, low])


def sine_matrix(depth):
    k = np.arange(1, depth + 1)
    return math.sqrt(2.0 / (depth + 1)) * np.sin(np.outer(k, k) * math.pi / (depth + 1))


def wave_table(depth, y_cells):
    k1 = y_cells // lanes
    ky = np.arange(k1)[:, None] + k1 * np.arange(lanes)[None, :]
    ey = 2.0 - 2.0 * np.cos(ky * 2.0 * math.pi / y_cells)
    ez = 2.0 - 2.0 * np.cos(np.arange(1, depth + 1) * math.pi / (depth + 1))
    return np.concatenate([ey, np.broadcast_to(ez[:, None], (depth, lanes))]).astype(np.float32)


def power(value, exponent):
    for _ in range(exponent.bit_length() - 1):
        value = value * value
    return value


def face(near, far, gain):
    return (far - near) + gain * (near + far)


def split_dot(rows, table_ref, pair, contract):
    count = rows.shape[0]
    high = rows.astype(jnp.bfloat16)
    low = (rows - high.astype(jnp.float32)).astype(jnp.bfloat16)

    def product(a, b):
        dims = (((1,), (contract,)), ((), ()))
        return lax.dot_general(a, b, dims, preferred_element_type=jnp.float32)

    main = product(jnp.concatenate([low, high], axis=0), table_ref[0, pair])
    return (product(high, table_ref[1, pair]) + main[:count]) + main[count:]


def halves(value):
    return value[:, :lanes], value[:, lanes:]


def to_modes(rhs, table_ref):
    f = [rhs[:, a * lanes : (a + 1) * lanes] for a in range(8)]
    s = [f[a] + f[a + 4] for a in range(4)]
    d = [f[a] - f[a + 4] for a in range(4)]
    u = diagonal * (d[1] - d[3])
    v = diagonal * (d[1] + d[3])
    even, odd = s[0] + s[2], s[1] + s[3]
    inputs = [
        (even + odd, even - odd),
        (d[0] + u, -(d[2] + v)),
        (s[0] - s[2], s[3] - s[1]),
        (d[0] - u, d[2] - v),
    ]
    blocks = [None] * 8
    for pair, columns in enumerate(inputs):
        out = split_dot(jnp.concatenate(columns, axis=1), table_ref, pair, 0)
        blocks[pair], blocks[8 - pair if pair else 4] = halves(out)
    return blocks


def from_modes(blocks, table_ref):
    outs = []
    for pair in range(4):
        columns = jnp.concatenate([blocks[pair], blocks[8 - pair if pair else 4]], axis=1)
        outs.append(halves(split_dot(columns, table_ref, pair, 1)))
    (p0, p4), (c1, q1), (c2, q2), (c3, q3) = outs
    even, odd = p0 + p4, p0 - p4
    m = diagonal * (c1 - c3)
    n = diagonal * (q1 + q3)
    both, other = c1 + c3, q1 - q3
    return [
        (even + c2) + both,
        (odd - q2) + (m - n),
        (even - c2) - other,
        (odd + q2) - (m + n),
        (even + c2) - both,
        (odd - q2) - (m - n),
        (even - c2) + other,
        (odd + q2) + (m + n),
    ]


def coefficients(diffusivity_ref, s):
    matrix = radau_matrix()
    d = diffusivity_ref[s]
    inverse, coef = [], []
    for i, row in enumerate(matrix):
        inverse.append(1.0 / (1.0 + (6.0 * step_size * row[i]) * d))
        coef.append([(step_size * entry) * d * inverse[i] for entry in row])
    return inverse, coef


def far_layer(n_z):
    return lax.axis_index("gz") % 2 * (n_z - 1)


def far_row(rows):
    return lax.axis_index("xy") % 2 * (rows - 1)


def pack_kernel(
    conc_hbm, pot_hbm, z_far_ref, z_near_ref, x_near_ref, x_far_ref, sems
):
    n_section, n_species, depth, rows, _ = conc_hbm.shape
    z_far = far_layer(depth)
    x_far = far_row(rows)
    copies = []
    for q, (z, ref) in enumerate(((z_far, z_far_ref), (depth - 1 - z_far, z_near_ref))):
        for j in range(n_section):
            pair = [
                pltpu.make_async_copy(
                    conc_hbm.at[j, :, z], ref.at[j, 0:n_species], sems.at[q, j, 0]
                ),
                pltpu.make_async_copy(pot_hbm.at[j, z], ref.at[j, n_species], sems.at[q, j, 1]),
            ]
            for copy in pair:
                copy.start()
            copies.extend(pair)
    for copy in copies:
        copy.wait()
    for x, out_ref in ((x_far, x_far_ref), (rows - 1 - x_far, x_near_ref)):
        for j in range(n_section):
            for q, ref in enumerate((z_far_ref, z_near_ref)):
                for s in range(n_species + 1):
                    to = edge_row(n_section, n_species, depth, j, s, q)
                    out_ref[to : to + 1, :] = ref[j, s, pl.ds(x, 1), :]


def edge_row(n_section, n_species, depth, j, s, q):
    if s < n_species:
        return (j * n_species + s) * depth + q
    return (n_section * n_species + j) * depth + q


def inner_kernel(
    diffusivity_ref, charge_ref, prev_ref, z_far_ref, z_near_ref, wave_ref,
    out_ref, decay_ref, own_ref, step_ref, between_ref,
):
    n_section, n_species, depth, rows, y_cells = out_ref.shape
    row = lax.broadcasted_iota(jnp.int32, (rows, y_cells), 0)
    layers = (z_far_ref, z_near_ref)
    z_far = far_layer(depth)
    for j in range(n_section):
        for q, ref in enumerate(layers):
            p = ref[j, n_species]
            step_ref[j, q, 0] = p - pltpu.roll(p, 1, 0)
            step_ref[j, q, 1] = pltpu.roll(p, y_cells - 1, 1) - p
        between_ref[j] = z_near_ref[j, n_species] - z_far_ref[j, n_species]

    def species(s, carry):
        half = 0.5 * charge_ref[s].astype(jnp.float32)
        inverse, coef = coefficients(diffusivity_ref, s)
        totals = []
        for j in range(n_section):
            planes = []
            for q, ref in enumerate(layers):
                c = ref[j, s]
                low = face(pltpu.roll(c, 1, 0), c, half * step_ref[j, q, 0])
                low = jnp.where(row == 0, 0.0, low)
                ahead = face(c, pltpu.roll(c, y_cells - 1, 1), half * step_ref[j, q, 1])
                planes.append(
                    (pltpu.roll(low, rows - 1, 0) - low) + (ahead - pltpu.roll(ahead, 1, 1))
                )
            between = face(z_far_ref[j, s], z_near_ref[j, s], half * between_ref[j])
            totals.append((planes[0] + between, planes[1] - between))
        for q, z in enumerate((z_far, depth - 1 - z_far)):
            prev = prev_ref[s, z]
            for i in range(n_section):
                c = layers[q][i, s]
                update = inverse[i] * (prev - c)
                for j in range(n_section):
                    update = update + coef[i][j] * totals[j][q]
                out_ref[i, s, q] = c + update
        return carry

    lax.fori_loop(0, n_species, species, 0)
    k1 = wave_ref.shape[0] - decay_ref.shape[1]
    lam = screening + wave_ref[pl.ds(lax.axis_index("gz"), 1), :] + wave_ref[k1:, :]
    root = jnp.sqrt(lam + 0.25 * lam * lam)
    r = 1.0 / (1.0 + 0.5 * lam + root)
    decay_ref[0] = r
    decay_ref[1] = 0.5 / root
    decay_ref[2] = power(r, rows)
    index = lax.axis_index("xy")
    solver = index // ring * group + index % group
    rho = decay_ref[2, pl.ds(solver, 1), :]
    own_ref[0:1, :] = rho
    own_ref[1:2, :] = 1.0 / (1.0 - power(rho, lax.axis_size("xy")))


def outer_kernel(
    diffusivity_ref, charge_ref, part_ref, z_far_ref, z_near_ref, z_far_got,
    x_far_sent, x_far_got, x_near_sent, x_near_got, z_near_got, table_ref,
    out_hbm, modes_ref, out_ref, rhs_ref, edge_ref, sems,
):
    n_section, n_species, depth, rows, y_cells = part_ref.shape
    planes = n_species * depth
    kind = lax.broadcasted_iota(jnp.int32, (planes, y_cells), 0) // depth
    by_row = [coefficients(diffusivity_ref, s)[1] for s in range(n_species)]

    def by_species(values):
        total = jnp.full((planes, y_cells), values[0], jnp.float32)
        for s in range(1, n_species):
            total = jnp.where(kind == s, values[s], total)
        return total

    half_rows = by_species([0.5 * charge_ref[s].astype(jnp.float32) for s in range(n_species)])
    sides = ((x_near_sent, x_near_got), (x_far_sent, x_far_got))
    faces = []
    for near, far in sides:
        for j in range(n_section):
            base = n_section * planes + j * depth
            step = far[base : base + depth, :] - near[base : base + depth, :]
            step = jnp.concatenate([step] * n_species, axis=0)
            at = slice(j * planes, (j + 1) * planes)
            faces.append(face(near[at, :], far[at, :], half_rows * step))
    for i in range(n_section):
        weights = [by_species([by_row[s][i][j] for s in range(n_species)]) for j in range(n_section)]
        for side in range(2):
            update = weights[0] * faces[side * n_section]
            for j in range(1, n_section):
                update = update + weights[j] * faces[side * n_section + j]
            edge_ref[side, i * planes : (i + 1) * planes, :] = update

    pairs = ((z_far_ref, z_far_got), (z_near_ref, z_near_got))
    for i in range(n_section):
        for q in range(depth):
            rhs_ref[i, q] = screening * pairs[q][0][i, n_species]
    row = lax.broadcasted_iota(jnp.int32, (rows, y_cells), 0)
    z_far = far_layer(depth)
    x_far = far_row(rows)
    at_x = (row == rows - 1 - x_far, row == x_far)

    def store(s, q):
        z = z_far if q == 0 else depth - 1 - z_far
        return pltpu.make_async_copy(out_ref.at[:, s, q], out_hbm.at[:, s, z], sems.at[s, q])

    def species(s, carry):
        half = 0.5 * charge_ref[s].astype(jnp.float32)
        _, coef = coefficients(diffusivity_ref, s)
        for q, (own, got) in enumerate(pairs):
            faces = []
            for j in range(n_section):
                step = got[j, n_species] - own[j, n_species]
                faces.append(face(own[j, s], got[j, s], half * step))
            for i in range(n_section):
                at = pl.ds(i * planes + s * depth + q, 1)
                update = part_ref[i, s, q]
                for side in range(2):
                    update = update + jnp.where(at_x[side], edge_ref[side, at, :], 0.0)
                for j in range(n_section):
                    update = update + coef[i][j] * faces[j]
                out_ref[i, s, q] = update
                rhs_ref[i, q] += (2.0 * half) * update
            store(s, q).start()
        return carry

    lax.fori_loop(0, n_species, species, 0)
    rhs = rhs_ref[...].reshape(n_section * depth * rows, y_cells)
    for g, block in enumerate(to_modes(rhs, table_ref)):
        modes_ref[g] = block
    for s in range(n_species):
        for q in range(depth):
            store(s, q).wait()


def layer_of(z, n_z):
    g = z // n_z
    return g, int(z % n_z != g % 2 * (n_z - 1))


def sine_rows(planes, table):
    depth = len(planes)
    half = depth // 2
    even = [planes[z] + planes[depth - 1 - z] for z in range(half)]
    odd = [planes[z] - planes[depth - 1 - z] for z in range(half)]
    out = []
    for k in range(depth):
        source = even if k % 2 == 0 else odd
        total = source[0] * float(table[k, 0])
        for z in range(1, half):
            total = total + source[z] * float(table[k, z])
        out.append(total)
    return out


def sine_rows_back(planes, table):
    depth = len(planes)
    out = [None] * depth
    for z in range(depth // 2):
        parts = []
        for parity in range(2):
            total = planes[parity] * float(table[parity, z])
            for k in range(parity + 2, depth, 2):
                total = total + planes[k] * float(table[k, z])
            parts.append(total)
        out[z] = parts[0] + parts[1]
        out[depth - 1 - z] = parts[0] - parts[1]
    return out


def sum_kernel(table, decay_ref, modes_ref, hat_ref, sums_ref, rows_ref):
    n_gz, n_section, n_z, rows, _ = modes_ref.shape
    depth = n_gz * n_z
    r = decay_ref[0]
    where = [layer_of(z, n_z) for z in range(depth)]
    for i in range(n_section):
        planes = [modes_ref[g, i, q] for g, q in where]
        for k, plane in enumerate(sine_rows(planes, table)):
            rows_ref[i, pl.ds(k * rows, rows), :] = plane
        for x in range(rows):
            hat_ref[i, x] = rows_ref[i, pl.ds(x, depth, stride=rows), :]
        ahead = hat_ref[i, 0]
        back = hat_ref[i, rows - 1]
        for x in range(1, rows):
            ahead = ahead * r + hat_ref[i, x]
            back = back * r + hat_ref[i, rows - 1 - x]
        for side, value in enumerate((ahead, back)):
            at = side * n_section + i
            for y in range(depth // group):
                four = value[y * group : (y + 1) * group]
                for copy in range(ring // group):
                    first = (y * ring + copy * group) * 2 * n_section + at
                    sums_ref[pl.ds(first, group, stride=2 * n_section), :] = four


def ring_kernel(n_section, own_ref, sums_ref, out_ref, all_ref):
    per = 2 * n_section
    n_xy = sums_ref.shape[0] // per
    rho = jnp.broadcast_to(own_ref[0:1, :], (n_section, lanes))
    scale = own_ref[1:2, :]

    def ahead_sum(d):
        return sums_ref[d * per : d * per + n_section, :]

    def back_sum(d):
        return sums_ref[d * per + n_section : (d + 1) * per, :]

    ahead = ahead_sum(0)
    back = back_sum(n_xy - 1)
    for d in range(1, n_xy):
        ahead = ahead * rho + ahead_sum(d)
        back = back * rho + back_sum(n_xy - 1 - d)
    ahead = ahead * scale
    back = back * scale
    for d in range(n_xy):
        e = n_xy - 1 - d
        all_ref[d * per : d * per + n_section, :] = ahead
        all_ref[e * per + n_section : (e + 1) * per, :] = back
        ahead = ahead * rho + ahead_sum(d)
        back = back * rho + back_sum(e)
    mine = lax.axis_index("xy") % ring // group
    span = group * per
    for y in range(n_xy // ring):
        first = pl.multiple_of(y * ring * per + mine * span, 8)
        out_ref[y * span : (y + 1) * span, :] = all_ref[pl.ds(first, span), :]


def solve_kernel(table, decay_ref, hat_ref, enter_ref, out_ref, work_ref, rows_ref):
    n_gz, n_section, n_z, rows, _ = out_ref.shape
    depth = n_gz * n_z
    r = decay_ref[0]
    inverse = decay_ref[1]
    where = [layer_of(z, n_z) for z in range(depth)]
    for i in range(n_section):
        value = enter_ref[pl.ds(i, depth, stride=2 * n_section), :]
        for x in range(rows):
            source = hat_ref[i, x]
            work_ref[x] = value * r
            value = value * r + source
        value = enter_ref[pl.ds(n_section + i, depth, stride=2 * n_section), :]
        for x in range(rows - 1, -1, -1):
            value = value * r + hat_ref[i, x]
            rows_ref[i, pl.ds(x, depth, stride=rows), :] = (work_ref[x] + value) * inverse
        planes = [rows_ref[i, pl.ds(k * rows, rows), :] for k in range(depth)]
        for (g, q), plane in zip(where, sine_rows_back(planes, table)):
            out_ref[g, i, q] = plane


def final_kernel(solved_ref, table_ref, out_ref):
    n_gz, n_section, n_z, rows, _ = solved_ref.shape
    z_far = far_layer(n_z)
    blocks = [solved_ref[g].reshape(n_section * n_z * rows, lanes) for g in range(n_gz)]
    for a, block in enumerate(from_modes(blocks, table_ref)):
        block = block.reshape(n_section, n_z, rows, lanes)
        for i in range(n_section):
            for q, z in enumerate((z_far, n_z - 1 - z_far)):
                out_ref[i, z, :, a * lanes : (a + 1) * lanes] = block[i, q]


def on_device(conc_prev, conc_section, potential, diffusivity, charges):
    n_xy = lax.axis_size("xy")
    n_gz = lax.axis_size("gz")
    n_section, n_species, n_z, rows, y_cells = conc_section.shape
    depth = n_z * n_gz
    f32 = jnp.float32
    vmem = pl.BlockSpec(memory_space=pltpu.VMEM)
    smem = pl.BlockSpec(memory_space=pltpu.SMEM)
    hbm = pl.BlockSpec(memory_space=pltpu.HBM)

    def params(mib):
        return pltpu.CompilerParams(vmem_limit_bytes=mib * 1024 * 1024)

    table = jnp.asarray(hartley_tables(y_cells))
    sine = sine_matrix(depth)
    wave = jnp.asarray(wave_table(depth, y_cells))

    layers = jax.ShapeDtypeStruct((n_section, n_species + 1, rows, y_cells), f32)
    edges = jax.ShapeDtypeStruct((n_section * n_z * (n_species + 1), y_cells), f32)
    z_far_out, z_near_out, x_near_out, x_far_out = pl.pallas_call(
        pack_kernel,
        out_shape=(layers, layers, edges, edges),
        in_specs=[hbm] * 2,
        out_specs=(vmem,) * 4,
        scratch_shapes=[pltpu.SemaphoreType.DMA((n_z, n_section, 2))],
        compiler_params=params(12),
        name="pack",
    )(
        pltpu.with_memory_space_constraint(conc_section, pltpu.HBM),
        pltpu.with_memory_space_constraint(potential, pltpu.HBM),
    )

    def swap(value, axis, pairs):
        return lax.ppermute(value, axis, pairs + [(j, i) for i, j in pairs])

    z_far_in = swap(z_far_out, "gz", [(i, i + 1) for i in range(1, n_gz - 1, 2)])
    x_far_in = swap(x_far_out, "xy", [(i, (i + 1) % n_xy) for i in range(1, n_xy, 2)])
    x_near_in = swap(x_near_out, "xy", [(i, i + 1) for i in range(0, n_xy, 2)])
    z_near_in = swap(z_near_out, "gz", [(i, i + 1) for i in range(0, n_gz, 2)])

    planes = (n_section, n_species, n_z, rows, y_cells)
    part, decay_here, own = pl.pallas_call(
        inner_kernel,
        out_shape=(
            jax.ShapeDtypeStruct(planes, f32),
            jax.ShapeDtypeStruct((3, depth, lanes), f32),
            jax.ShapeDtypeStruct((2, lanes), f32),
        ),
        in_specs=[smem] * 2 + [vmem] * 4,
        out_specs=(vmem, vmem, vmem),
        scratch_shapes=[
            pltpu.VMEM((n_section, n_z, 2, rows, y_cells), f32),
            pltpu.VMEM((n_section, rows, y_cells), f32),
        ],
        compiler_params=params(24),
        cost_estimate=pl.CostEstimate(flops=20_000_000, bytes_accessed=4_500_000, transcendentals=0),
        name="inner_faces",
    )(diffusivity, charges, conc_prev, z_far_out, z_near_out, wave)

    conc_new, modes = pl.pallas_call(
        outer_kernel,
        out_shape=(
            jax.ShapeDtypeStruct(conc_section.shape, f32),
            jax.ShapeDtypeStruct((n_gz, n_section * n_z * rows, lanes), f32),
        ),
        in_specs=[smem] * 2 + [vmem] * 10,
        out_specs=(hbm, vmem),
        scratch_shapes=[
            pltpu.VMEM(planes, f32),
            pltpu.VMEM((n_section, n_z, rows, y_cells), f32),
            pltpu.VMEM((2, n_section * n_species * n_z, y_cells), f32),
            pltpu.SemaphoreType.DMA((n_species, n_z)),
        ],
        compiler_params=params(24),
        name="outer_faces",
    )(
        diffusivity, charges, part, z_far_out, z_near_out, z_far_in,
        x_far_out, x_far_in, x_near_out, x_near_in, z_near_in, table,
    )

    columns = lax.all_to_all(modes, "gz", split_axis=0, concat_axis=0, tiled=True)
    columns = columns.reshape(n_gz, n_section, n_z, rows, lanes)

    n_rows = 2 * n_section * n_xy
    hat, sums = pl.pallas_call(
        functools.partial(sum_kernel, sine),
        out_shape=(
            jax.ShapeDtypeStruct((n_section, rows, depth, lanes), f32),
            jax.ShapeDtypeStruct((n_rows, lanes), f32),
        ),
        in_specs=[vmem] * 2,
        out_specs=(vmem, vmem),
        scratch_shapes=[pltpu.VMEM((n_section, depth * rows, lanes), f32)],
        compiler_params=params(12),
        name="block_sums",
    )(decay_here, columns)

    sums = sums.reshape(n_xy, n_section, 2, lanes)
    gathered = lax.all_to_all(sums, "xy", split_axis=0, concat_axis=0, tiled=True)
    gathered = gathered.reshape(n_rows, lanes)
    entering = pl.pallas_call(
        functools.partial(ring_kernel, n_section),
        out_shape=jax.ShapeDtypeStruct((2 * n_section * depth, lanes), f32),
        in_specs=[vmem] * 2,
        out_specs=vmem,
        scratch_shapes=[pltpu.VMEM((n_rows, lanes), f32)],
        compiler_params=params(12),
        name="ring",
    )(own, gathered)
    sharers = [
        [y * ring + first + z for y in range(n_xy // ring) for z in range(group)]
        for first in range(0, ring, group)
    ]
    entering = entering.reshape(depth, n_section, 2, lanes)
    enter = lax.all_to_all(
        entering, "xy", split_axis=0, concat_axis=0, tiled=True, axis_index_groups=sharers
    )
    enter = enter.reshape(2 * n_section * depth, lanes)

    solved = pl.pallas_call(
        functools.partial(solve_kernel, sine),
        out_shape=jax.ShapeDtypeStruct((n_gz, n_section, n_z, rows, lanes), f32),
        in_specs=[vmem] * 3,
        out_specs=vmem,
        scratch_shapes=[
            pltpu.VMEM((rows, depth, lanes), f32),
            pltpu.VMEM((n_section, depth * rows, lanes), f32),
        ],
        compiler_params=params(12),
        name="solve",
    )(decay_here, hat, enter)
    returned = lax.all_to_all(solved, "gz", split_axis=0, concat_axis=0, tiled=True)

    potential_new = pl.pallas_call(
        final_kernel,
        out_shape=jax.ShapeDtypeStruct(potential.shape, f32),
        in_specs=[vmem] * 2,
        out_specs=vmem,
        compiler_params=params(12),
        name="back_to_y",
    )(returned, table)
    return (conc_new, potential_new)


def solution(mesh):
    in_specs = (
        P(None, "gz", "xy", None),
        P(None, None, "gz", "xy", None),
        P(None, "gz", "xy", None),
        P(),
        P(),
    )
    out_specs = (P(None, None, "gz", "xy", None), P(None, "gz", "xy", None))
    return jax.shard_map(
        on_device, mesh=mesh, in_specs=in_specs, out_specs=out_specs, check_vma=False
    )
```

```python
import functools
import math

import jax
import jax.numpy as jnp
import numpy as np
from jax import lax
from jax.experimental import pallas as pl
from jax.experimental.pallas import tpu as pltpu
from jax.sharding import PartitionSpec as P

step_size = 0.2
screening = 0.005
lanes = 128
ring = 16
group = 4
diagonal = math.sqrt(0.5)


def radau_matrix():
    root = math.sqrt(6.0)
    return [
        [(88.0 - 7.0 * root) / 360.0, (296.0 - 169.0 * root) / 1800.0, (-2.0 + 3.0 * root) / 225.0],
        [(296.0 + 169.0 * root) / 1800.0, (88.0 + 7.0 * root) / 360.0, (-2.0 - 3.0 * root) / 225.0],
        [(16.0 - root) / 36.0, (16.0 + root) / 36.0, 1.0 / 9.0],
    ]


def hartley_tables(length):
    b = np.arange(lanes)
    k1 = np.arange(length // lanes)[:, None, None]
    angle = b[:, None] * (k1 + length // lanes * b[None, :]) % length * (2.0 * math.pi / length)
    cas, dif = np.cos(angle) + np.sin(angle), np.sin(angle) - np.cos(angle)
    zero = np.zeros((lanes, lanes))
    pairs = [np.block([[cas[0], zero], [zero, cas[4]]])]
    pairs += [np.block([[cas[p], cas[8 - p]], [dif[p], -dif[8 - p]]]) for p in (1, 2, 3)]
    table = (np.stack(pairs) / math.sqrt(length)).astype(np.float32)
    high = table.astype(jnp.bfloat16)
    low = (table - high.astype(np.float32)).astype(jnp.bfloat16)
    return np.stack([high, low])


def sine_matrix(depth):
    k = np.arange(1, depth + 1)
    return math.sqrt(2.0 / (depth + 1)) * np.sin(np.outer(k, k) * math.pi / (depth + 1))


def wave_table(depth, y_cells):
    k1 = y_cells // lanes
    ky = np.arange(k1)[:, None] + k1 * np.arange(lanes)[None, :]
    ey = 2.0 - 2.0 * np.cos(ky * 2.0 * math.pi / y_cells)
    ez = 2.0 - 2.0 * np.cos(np.arange(1, depth + 1) * math.pi / (depth + 1))
    return np.concatenate([ey, np.broadcast_to(ez[:, None], (depth, lanes))]).astype(np.float32)


def power(value, exponent):
    for _ in range(exponent.bit_length() - 1):
        value = value * value
    return value


def face(near, far, gain):
    return (far - near) + gain * (near + far)


def split_dot(rows, table_ref, pair):
    count = rows.shape[0]
    high = rows.astype(jnp.bfloat16)
    low = (rows - high.astype(jnp.float32)).astype(jnp.bfloat16)

    def product(a, b):
        return jnp.dot(a, b, preferred_element_type=jnp.float32)

    main = product(jnp.concatenate([low, high], axis=0), table_ref[0, pair])
    return (product(high, table_ref[1, pair]) + main[:count]) + main[count:]


def halves(value):
    return value[:, :lanes], value[:, lanes:]


def to_modes(rhs, table_ref):
    f = [rhs[:, a * lanes : (a + 1) * lanes] for a in range(8)]
    s = [f[a] + f[a + 4] for a in range(4)]
    d = [f[a] - f[a + 4] for a in range(4)]
    u = diagonal * (d[1] - d[3])
    v = diagonal * (d[1] + d[3])
    even, odd = s[0] + s[2], s[1] + s[3]
    inputs = [
        (even + odd, even - odd),
        (d[0] + u, -(d[2] + v)),
        (s[0] - s[2], s[3] - s[1]),
        (d[0] - u, d[2] - v),
    ]
    blocks = [None] * 8
    for pair, columns in enumerate(inputs):
        out = split_dot(jnp.concatenate(columns, axis=1), table_ref, pair)
        blocks[pair], blocks[8 - pair if pair else 4] = halves(out)
    return blocks


def from_modes(blocks, table_ref):
    outs = []
    for pair in range(4):
        columns = jnp.concatenate([blocks[pair], blocks[8 - pair if pair else 4]], axis=1)
        outs.append(halves(split_dot(columns, table_ref, pair)))
    (p0, p4), (c1, q1), (c2, q2), (c3, q3) = outs
    even, odd = p0 + p4, p0 - p4
    m = diagonal * (c1 - c3)
    n = diagonal * (q1 + q3)
    both, other = c1 + c3, q1 - q3
    return [
        (even + c2) + both,
        (odd - q2) + (m - n),
        (even - c2) - other,
        (odd + q2) - (m + n),
        (even + c2) - both,
        (odd - q2) - (m - n),
        (even - c2) + other,
        (odd + q2) + (m + n),
    ]


def coefficients(diffusivity_ref, s):
    matrix = radau_matrix()
    d = diffusivity_ref[s]
    inverse, coef = [], []
    for i, row in enumerate(matrix):
        inverse.append(1.0 / (1.0 + (6.0 * step_size * row[i]) * d))
        coef.append([(step_size * entry) * d * inverse[i] for entry in row])
    return inverse, coef


def far_layer(n_z):
    return lax.axis_index("gz") % 2 * (n_z - 1)


def far_row(rows):
    return lax.axis_index("xy") % 2 * (rows - 1)


def pack_kernel(
    conc_hbm, pot_hbm, z_far_ref, z_near_ref, x_near_ref, x_far_ref, sems
):
    n_section, n_species, depth, rows, _ = conc_hbm.shape
    z_far = far_layer(depth)
    x_far = far_row(rows)
    layers = ((z_far, z_far_ref), (depth - 1 - z_far, z_near_ref))
    copies = []
    for j in range(n_section):
        copies.append([])
        for q, (z, ref) in enumerate(layers):
            copies[j] += [
                pltpu.make_async_copy(
                    conc_hbm.at[j, :, z], ref.at[j, 0:n_species], sems.at[q, j, 0]
                ),
                pltpu.make_async_copy(pot_hbm.at[j, z], ref.at[j, n_species], sems.at[q, j, 1]),
            ]
        for copy in copies[j]:
            copy.start()
    for j in range(n_section):
        for copy in copies[j]:
            copy.wait()
        for x, out_ref in ((x_far, x_far_ref), (rows - 1 - x_far, x_near_ref)):
            for q, (_, ref) in enumerate(layers):
                for s in range(n_species + 1):
                    to = edge_row(n_section, n_species, depth, j, s, q)
                    out_ref[to : to + 1, :] = ref[j, s, pl.ds(x, 1), :]


def edge_row(n_section, n_species, depth, j, s, q):
    if s < n_species:
        return (j * n_species + s) * depth + q
    return (n_section * n_species + j) * depth + q


def inner_kernel(
    diffusivity_ref, charge_ref, prev_ref, z_far_ref, z_near_ref, wave_ref,
    out_ref, rhs_ref, decay_ref, own_ref, step_ref, between_ref,
):
    n_section, n_species, depth, rows, y_cells = out_ref.shape
    row = lax.broadcasted_iota(jnp.int32, (rows, y_cells), 0)
    layers = (z_far_ref, z_near_ref)
    z_far = far_layer(depth)
    for j in range(n_section):
        for q, ref in enumerate(layers):
            p = ref[j, n_species]
            step_ref[j, q, 0] = p - pltpu.roll(p, 1, 0)
            step_ref[j, q, 1] = pltpu.roll(p, y_cells - 1, 1) - p
            rhs_ref[j, q] = screening * p
        between_ref[j] = z_near_ref[j, n_species] - z_far_ref[j, n_species]

    def species(s, carry):
        half = 0.5 * charge_ref[s].astype(jnp.float32)
        inverse, coef = coefficients(diffusivity_ref, s)
        totals = []
        for j in range(n_section):
            planes = []
            for q, ref in enumerate(layers):
                c = ref[j, s]
                low = face(pltpu.roll(c, 1, 0), c, half * step_ref[j, q, 0])
                low = jnp.where(row == 0, 0.0, low)
                ahead = face(c, pltpu.roll(c, y_cells - 1, 1), half * step_ref[j, q, 1])
                planes.append(
                    (pltpu.roll(low, rows - 1, 0) - low) + (ahead - pltpu.roll(ahead, 1, 1))
                )
            between = face(z_far_ref[j, s], z_near_ref[j, s], half * between_ref[j])
            totals.append((planes[0] + between, planes[1] - between))
        for q, z in enumerate((z_far, depth - 1 - z_far)):
            prev = prev_ref[s, z]
            for i in range(n_section):
                c = layers[q][i, s]
                update = inverse[i] * (prev - c)
                for j in range(n_section):
                    update = update + coef[i][j] * totals[j][q]
                update = c + update
                out_ref[i, s, q] = update
                rhs_ref[i, q] += (2.0 * half) * update
        return carry

    lax.fori_loop(0, n_species, species, 0)
    k1 = wave_ref.shape[0] - decay_ref.shape[1]
    lam = screening + wave_ref[pl.ds(lax.axis_index("gz"), 1), :] + wave_ref[k1:, :]
    root = jnp.sqrt(lam + 0.25 * lam * lam)
    r = 1.0 / (1.0 + 0.5 * lam + root)
    decay_ref[0] = r
    decay_ref[1] = 0.5 / root
    decay_ref[2] = power(r, rows)
    index = lax.axis_index("xy")
    solver = index // ring * group + index % group
    rho = decay_ref[2, pl.ds(solver, 1), :]
    own_ref[0:1, :] = rho
    own_ref[1:2, :] = 1.0 / (1.0 - power(rho, lax.axis_size("xy")))


def outer_kernel(
    diffusivity_ref, charge_ref, part_ref, rhs_part_ref, z_far_ref, z_near_ref, z_far_got,
    x_far_sent, x_far_got, x_near_sent, x_near_got, z_near_got, table_ref,
    out_hbm, modes_ref, out_ref, rhs_ref, edge_ref, step_ref, sems,
):
    n_section, n_species, depth, rows, y_cells = part_ref.shape
    planes = n_species * depth
    pairs = ((z_far_ref, z_far_got), (z_near_ref, z_near_got))
    charge = [charge_ref[s].astype(jnp.float32) for s in range(n_species)]
    kind = lax.broadcasted_iota(jnp.int32, (planes, y_cells), 0) // depth
    by_row = [coefficients(diffusivity_ref, s)[1] for s in range(n_species)]
    z_far = far_layer(depth)
    x_far = far_row(rows)

    def by_species(values):
        total = jnp.full((planes, y_cells), values[0], jnp.float32)
        for s in range(1, n_species):
            total = jnp.where(kind == s, values[s], total)
        return total

    for i in range(n_section):
        for q, (own, got) in enumerate(pairs):
            step_ref[i, q] = got[i, n_species] - own[i, n_species]
            rhs_ref[i, q] = rhs_part_ref[i, q]
    charge_rows = by_species(charge)
    sides = ((x_near_sent, x_near_got), (x_far_sent, x_far_got))
    faces = []
    for near, far in sides:
        for j in range(n_section):
            base = n_section * planes + j * depth
            step = far[base : base + depth, :] - near[base : base + depth, :]
            step = jnp.concatenate([step] * n_species, axis=0)
            at = slice(j * planes, (j + 1) * planes)
            faces.append(face(near[at, :], far[at, :], 0.5 * charge_rows * step))
    edge_rows = (rows - 1 - x_far, x_far)
    for i in range(n_section):
        weights = [by_species([by_row[s][i][j] for s in range(n_species)]) for j in range(n_section)]
        for side, x in enumerate(edge_rows):
            update = weights[0] * faces[side * n_section]
            for j in range(1, n_section):
                update = update + weights[j] * faces[side * n_section + j]
            edge_ref[side, i * planes : (i + 1) * planes, :] = update
            update = charge_rows * update
            total = update[0:depth]
            for s in range(1, n_species):
                total = total + update[s * depth : (s + 1) * depth]
            for q in range(depth):
                rhs_ref[i, q, pl.ds(x, 1), :] += total[q : q + 1]

    def store(s, q):
        z = z_far if q == 0 else depth - 1 - z_far
        return pltpu.make_async_copy(out_ref.at[:, s, q], out_hbm.at[:, s, z], sems.at[s, q])

    def species(s, carry):
        q_s = charge_ref[s].astype(jnp.float32)
        half = 0.5 * q_s
        _, coef = coefficients(diffusivity_ref, s)
        for q, (own, got) in enumerate(pairs):
            faces = [face(own[j, s], got[j, s], half * step_ref[j, q]) for j in range(n_section)]
            for i in range(n_section):
                update = coef[i][0] * faces[0]
                for j in range(1, n_section):
                    update = update + coef[i][j] * faces[j]
                out_ref[i, s, q] = part_ref[i, s, q] + update
                rhs_ref[i, q] += q_s * update
                at = pl.ds((i * n_species + s) * depth + q, 1)
                for side, x in enumerate(edge_rows):
                    out_ref[i, s, q, pl.ds(x, 1), :] += edge_ref[side, at, :]
            store(s, q).start()
        return carry

    lax.fori_loop(0, n_species, species, 0)
    rhs = rhs_ref[...].reshape(n_section * depth * rows, y_cells)
    for g, block in enumerate(to_modes(rhs, table_ref)):
        modes_ref[g] = block
    for s in range(n_species):
        for q in range(depth):
            store(s, q).wait()


def layer_of(z, n_z):
    g = z // n_z
    return g, int(z % n_z != g % 2 * (n_z - 1))


def sine_rows(planes, table):
    depth = len(planes)
    half = depth // 2
    even = [planes[z] + planes[depth - 1 - z] for z in range(half)]
    odd = [planes[z] - planes[depth - 1 - z] for z in range(half)]
    out = []
    for k in range(depth):
        source = even if k % 2 == 0 else odd
        total = source[0] * float(table[k, 0])
        for z in range(1, half):
            total = total + source[z] * float(table[k, z])
        out.append(total)
    return out


def sine_rows_back(planes, table):
    depth = len(planes)
    out = [None] * depth
    for z in range(depth // 2):
        parts = []
        for parity in range(2):
            total = planes[parity] * float(table[parity, z])
            for k in range(parity + 2, depth, 2):
                total = total + planes[k] * float(table[k, z])
            parts.append(total)
        out[z] = parts[0] + parts[1]
        out[depth - 1 - z] = parts[0] - parts[1]
    return out


def sum_kernel(table, decay_ref, modes_ref, hat_ref, sums_ref, rows_ref):
    n_gz, n_section, n_z, rows, _ = modes_ref.shape
    depth = n_gz * n_z
    r = decay_ref[0]
    where = [layer_of(z, n_z) for z in range(depth)]
    for i in range(n_section):
        planes = [modes_ref[g, i, q] for g, q in where]
        for k, plane in enumerate(sine_rows(planes, table)):
            rows_ref[i, pl.ds(k * rows, rows), :] = plane
        for x in range(rows):
            hat_ref[i, x] = rows_ref[i, pl.ds(x, depth, stride=rows), :]
        ahead = hat_ref[i, 0]
        back = hat_ref[i, rows - 1]
        for x in range(1, rows):
            ahead = ahead * r + hat_ref[i, x]
            back = back * r + hat_ref[i, rows - 1 - x]
        for side, value in enumerate((ahead, back)):
            at = side * n_section + i
            for y in range(depth // group):
                four = value[y * group : (y + 1) * group]
                for copy in range(ring // group):
                    first = (y * ring + copy * group) * 2 * n_section + at
                    sums_ref[pl.ds(first, group, stride=2 * n_section), :] = four


def ring_kernel(n_section, own_ref, sums_ref, out_ref, all_ref):
    per = 2 * n_section
    n_rings = sums_ref.shape[0] // (per * ring)
    rho = jnp.broadcast_to(own_ref[0:1, :], (n_section, lanes))
    around = power(rho, ring)
    scale = own_ref[1:2, :]

    def ahead_sum(y, z):
        at = (y * ring + z) * per
        return sums_ref[at : at + n_section, :]

    def back_sum(y, z):
        at = (y * ring + z) * per + n_section
        return sums_ref[at : at + n_section, :]

    ahead, back = [], []
    for y in range(n_rings):
        forth, aback = ahead_sum(y, 0), back_sum(y, ring - 1)
        for z in range(1, ring):
            forth = forth * rho + ahead_sum(y, z)
            aback = aback * rho + back_sum(y, ring - 1 - z)
        ahead.append(forth)
        back.append(aback)
    for y in range(n_rings):
        forth, aback = ahead[y], back[y]
        for distance in range(n_rings - 1, 0, -1):
            forth = forth * around + ahead[(y - distance) % n_rings]
            aback = aback * around + back[(y + distance) % n_rings]
        forth, aback = forth * scale, aback * scale
        for z in range(ring):
            at = (y * ring + z) * per
            all_ref[at : at + n_section, :] = forth
            forth = forth * rho + ahead_sum(y, z)
            e = ring - 1 - z
            at = (y * ring + e) * per + n_section
            all_ref[at : at + n_section, :] = aback
            aback = aback * rho + back_sum(y, e)
    mine = lax.axis_index("xy") % ring // group
    span = group * per
    for y in range(n_rings):
        first = pl.multiple_of(y * ring * per + mine * span, 8)
        out_ref[y * span : (y + 1) * span, :] = all_ref[pl.ds(first, span), :]


def solve_kernel(table, decay_ref, hat_ref, enter_ref, out_ref, work_ref, rows_ref):
    n_gz, n_section, n_z, rows, _ = out_ref.shape
    depth = n_gz * n_z
    r = decay_ref[0]
    inverse = decay_ref[1]
    where = [layer_of(z, n_z) for z in range(depth)]
    for i in range(n_section):
        value = enter_ref[pl.ds(i, depth, stride=2 * n_section), :]
        for x in range(rows):
            source = hat_ref[i, x]
            work_ref[x] = value * r
            value = value * r + source
        value = enter_ref[pl.ds(n_section + i, depth, stride=2 * n_section), :]
        for x in range(rows - 1, -1, -1):
            value = value * r + hat_ref[i, x]
            rows_ref[i, pl.ds(x, depth, stride=rows), :] = (work_ref[x] + value) * inverse
        planes = [rows_ref[i, pl.ds(k * rows, rows), :] for k in range(depth)]
        for (g, q), plane in zip(where, sine_rows_back(planes, table)):
            out_ref[g, i, q] = plane


def final_kernel(solved_ref, table_ref, out_hbm, out_ref, sems):
    n_gz, n_section, n_z, rows, _ = solved_ref.shape
    z_far = far_layer(n_z)
    blocks = [solved_ref[g].reshape(n_section * n_z * rows, lanes) for g in range(n_gz)]
    fields = from_modes(blocks, table_ref)
    copies = []
    for i in range(n_section):
        for q, z in enumerate((z_far, n_z - 1 - z_far)):
            at = (i * n_z + q) * rows
            for a, field in enumerate(fields):
                out_ref[i, q, :, a * lanes : (a + 1) * lanes] = field[at : at + rows]
            copies.append(
                pltpu.make_async_copy(out_ref.at[i, q], out_hbm.at[i, z], sems.at[i, q])
            )
            copies[-1].start()
    for copy in copies:
        copy.wait()


def on_device(conc_prev, conc_section, potential, diffusivity, charges):
    n_xy = lax.axis_size("xy")
    n_gz = lax.axis_size("gz")
    n_section, n_species, n_z, rows, y_cells = conc_section.shape
    depth = n_z * n_gz
    f32 = jnp.float32
    vmem = pl.BlockSpec(memory_space=pltpu.VMEM)
    smem = pl.BlockSpec(memory_space=pltpu.SMEM)
    hbm = pl.BlockSpec(memory_space=pltpu.HBM)

    def params(mib):
        return pltpu.CompilerParams(vmem_limit_bytes=mib * 1024 * 1024)

    tables = hartley_tables(y_cells)
    table, table_back = jnp.asarray(tables), jnp.asarray(tables.swapaxes(2, 3))
    sine = sine_matrix(depth)
    wave = jnp.asarray(wave_table(depth, y_cells))

    layers = jax.ShapeDtypeStruct((n_section, n_species + 1, rows, y_cells), f32)
    edges = jax.ShapeDtypeStruct((n_section * n_z * (n_species + 1), y_cells), f32)
    z_far_out, z_near_out, x_near_out, x_far_out = pl.pallas_call(
        pack_kernel,
        out_shape=(layers, layers, edges, edges),
        in_specs=[hbm] * 2,
        out_specs=(vmem,) * 4,
        scratch_shapes=[pltpu.SemaphoreType.DMA((n_z, n_section, 2))],
        compiler_params=params(12),
        name="pack",
    )(
        pltpu.with_memory_space_constraint(conc_section, pltpu.HBM),
        pltpu.with_memory_space_constraint(potential, pltpu.HBM),
    )

    def swap(value, axis, pairs):
        return lax.ppermute(value, axis, pairs + [(j, i) for i, j in pairs])

    z_far_in = swap(z_far_out, "gz", [(i, i + 1) for i in range(1, n_gz - 1, 2)])
    x_far_in = swap(x_far_out, "xy", [(i, (i + 1) % n_xy) for i in range(1, n_xy, 2)])
    x_near_in = swap(x_near_out, "xy", [(i, i + 1) for i in range(0, n_xy, 2)])
    z_near_in = swap(z_near_out, "gz", [(i, i + 1) for i in range(0, n_gz, 2)])

    planes = (n_section, n_species, n_z, rows, y_cells)
    rhs_shape = (n_section, n_z, rows, y_cells)
    part, rhs_part, decay_here, own = pl.pallas_call(
        inner_kernel,
        out_shape=(
            jax.ShapeDtypeStruct(planes, f32),
            jax.ShapeDtypeStruct(rhs_shape, f32),
            jax.ShapeDtypeStruct((3, depth, lanes), f32),
            jax.ShapeDtypeStruct((2, lanes), f32),
        ),
        in_specs=[smem] * 2 + [vmem] * 4,
        out_specs=(vmem,) * 4,
        scratch_shapes=[
            pltpu.VMEM((n_section, n_z, 2, rows, y_cells), f32),
            pltpu.VMEM((n_section, rows, y_cells), f32),
        ],
        compiler_params=params(24),
        cost_estimate=pl.CostEstimate(flops=20_000_000, bytes_accessed=4_500_000, transcendentals=0),
        name="inner_faces",
    )(diffusivity, charges, conc_prev, z_far_out, z_near_out, wave)

    conc_new, modes = pl.pallas_call(
        outer_kernel,
        out_shape=(
            jax.ShapeDtypeStruct(conc_section.shape, f32),
            jax.ShapeDtypeStruct((n_gz, n_section * n_z * rows, lanes), f32),
        ),
        in_specs=[smem] * 2 + [vmem] * 11,
        out_specs=(hbm, vmem),
        scratch_shapes=[
            pltpu.VMEM(planes, f32),
            pltpu.VMEM(rhs_shape, f32),
            pltpu.VMEM((2, n_section * n_species * n_z, y_cells), f32),
            pltpu.VMEM(rhs_shape, f32),
            pltpu.SemaphoreType.DMA((n_species, n_z)),
        ],
        compiler_params=params(24),
        name="outer_faces",
    )(
        diffusivity, charges, part, rhs_part, z_far_out, z_near_out, z_far_in,
        x_far_out, x_far_in, x_near_out, x_near_in, z_near_in, table,
    )

    columns = lax.all_to_all(modes, "gz", split_axis=0, concat_axis=0, tiled=True)
    columns = columns.reshape(n_gz, n_section, n_z, rows, lanes)

    n_rows = 2 * n_section * n_xy
    hat, sums = pl.pallas_call(
        functools.partial(sum_kernel, sine),
        out_shape=(
            jax.ShapeDtypeStruct((n_section, rows, depth, lanes), f32),
            jax.ShapeDtypeStruct((n_rows, lanes), f32),
        ),
        in_specs=[vmem] * 2,
        out_specs=(vmem, vmem),
        scratch_shapes=[pltpu.VMEM((n_section, depth * rows, lanes), f32)],
        compiler_params=params(12),
        name="block_sums",
    )(decay_here, columns)

    sums = sums.reshape(n_xy, n_section, 2, lanes)
    gathered = lax.all_to_all(sums, "xy", split_axis=0, concat_axis=0, tiled=True)
    gathered = gathered.reshape(n_rows, lanes)
    entering = pl.pallas_call(
        functools.partial(ring_kernel, n_section),
        out_shape=jax.ShapeDtypeStruct((2 * n_section * depth, lanes), f32),
        in_specs=[vmem] * 2,
        out_specs=vmem,
        scratch_shapes=[pltpu.VMEM((n_rows, lanes), f32)],
        compiler_params=params(12),
        name="ring",
    )(own, gathered)
    sharers = [
        [y * ring + first + z for y in range(n_xy // ring) for z in range(group)]
        for first in range(0, ring, group)
    ]
    entering = entering.reshape(depth, n_section, 2, lanes)
    enter = lax.all_to_all(
        entering, "xy", split_axis=0, concat_axis=0, tiled=True, axis_index_groups=sharers
    )
    enter = enter.reshape(2 * n_section * depth, lanes)

    solved = pl.pallas_call(
        functools.partial(solve_kernel, sine),
        out_shape=jax.ShapeDtypeStruct((n_gz, n_section, n_z, rows, lanes), f32),
        in_specs=[vmem] * 3,
        out_specs=vmem,
        scratch_shapes=[
            pltpu.VMEM((rows, depth, lanes), f32),
            pltpu.VMEM((n_section, depth * rows, lanes), f32),
        ],
        compiler_params=params(12),
        name="solve",
    )(decay_here, hat, enter)
    returned = lax.all_to_all(solved, "gz", split_axis=0, concat_axis=0, tiled=True)

    potential_new = pl.pallas_call(
        final_kernel,
        out_shape=jax.ShapeDtypeStruct(potential.shape, f32),
        in_specs=[vmem] * 2,
        out_specs=hbm,
        scratch_shapes=[
            pltpu.VMEM(potential.shape, f32),
            pltpu.SemaphoreType.DMA((n_section, n_z)),
        ],
        compiler_params=params(12),
        name="back_to_y",
    )(returned, table_back)
    return (conc_new, potential_new)


def solution(mesh):
    in_specs = (
        P(None, "gz", "xy", None),
        P(None, None, "gz", "xy", None),
        P(None, "gz", "xy", None),
        P(),
        P(),
    )
    out_specs = (P(None, None, "gz", "xy", None), P(None, "gz", "xy", None))
    return jax.shard_map(
        on_device, mesh=mesh, in_specs=in_specs, out_specs=out_specs, check_vma=False
    )
```

```python
import functools
import math

import jax
import jax.numpy as jnp
import numpy as np
from jax import lax
from jax.experimental import pallas as pl
from jax.experimental.pallas import tpu as pltpu
from jax.sharding import PartitionSpec as P

step_size = 0.2
screening = 0.005
lanes = 128
ring = 16
group = 4
diagonal = math.sqrt(0.5)


def radau_matrix():
    root = math.sqrt(6.0)
    return [
        [(88.0 - 7.0 * root) / 360.0, (296.0 - 169.0 * root) / 1800.0, (-2.0 + 3.0 * root) / 225.0],
        [(296.0 + 169.0 * root) / 1800.0, (88.0 + 7.0 * root) / 360.0, (-2.0 - 3.0 * root) / 225.0],
        [(16.0 - root) / 36.0, (16.0 + root) / 36.0, 1.0 / 9.0],
    ]


def hartley_tables(length):
    b = np.arange(lanes)
    k1 = np.arange(length // lanes)[:, None, None]
    angle = b[:, None] * (k1 + length // lanes * b[None, :]) % length * (2.0 * math.pi / length)
    cas, dif = np.cos(angle) + np.sin(angle), np.sin(angle) - np.cos(angle)
    zero = np.zeros((lanes, lanes))
    pairs = [np.block([[cas[0], zero], [zero, cas[4]]])]
    pairs += [np.block([[cas[p], cas[8 - p]], [dif[p], -dif[8 - p]]]) for p in (1, 2, 3)]
    table = (np.stack(pairs) / math.sqrt(length)).astype(np.float32)
    high = table.astype(jnp.bfloat16)
    low = (table - high.astype(np.float32)).astype(jnp.bfloat16)
    return np.stack([high, low])


def sine_matrix(depth):
    k = np.arange(1, depth + 1)
    return math.sqrt(2.0 / (depth + 1)) * np.sin(np.outer(k, k) * math.pi / (depth + 1))


def wave_table(depth, y_cells):
    k1 = y_cells // lanes
    ky = np.arange(k1)[:, None] + k1 * np.arange(lanes)[None, :]
    ey = 2.0 - 2.0 * np.cos(ky * 2.0 * math.pi / y_cells)
    ez = 2.0 - 2.0 * np.cos(np.arange(1, depth + 1) * math.pi / (depth + 1))
    return np.concatenate([ey, np.broadcast_to(ez[:, None], (depth, lanes))]).astype(np.float32)


def power(value, exponent):
    for _ in range(exponent.bit_length() - 1):
        value = value * value
    return value


def face(near, far, gain):
    return (far - near) + gain * (near + far)


def split_dot(rows, table_ref, pair):
    count = rows.shape[0]
    high = rows.astype(jnp.bfloat16)
    low = (rows - high.astype(jnp.float32)).astype(jnp.bfloat16)

    def product(a, b):
        return jnp.dot(a, b, preferred_element_type=jnp.float32)

    main = product(jnp.concatenate([low, high], axis=0), table_ref[0, pair])
    return (product(high, table_ref[1, pair]) + main[:count]) + main[count:]


def halves(value):
    return value[:, :lanes], value[:, lanes:]


def to_modes(rhs, table_ref):
    f = [rhs[:, a * lanes : (a + 1) * lanes] for a in range(8)]
    s = [f[a] + f[a + 4] for a in range(4)]
    d = [f[a] - f[a + 4] for a in range(4)]
    u = diagonal * (d[1] - d[3])
    v = diagonal * (d[1] + d[3])
    even, odd = s[0] + s[2], s[1] + s[3]
    inputs = [
        (even + odd, even - odd),
        (d[0] + u, -(d[2] + v)),
        (s[0] - s[2], s[3] - s[1]),
        (d[0] - u, d[2] - v),
    ]
    blocks = [None] * 8
    for pair, columns in enumerate(inputs):
        out = split_dot(jnp.concatenate(columns, axis=1), table_ref, pair)
        blocks[pair], blocks[8 - pair if pair else 4] = halves(out)
    return blocks


def from_modes(blocks, table_ref):
    outs = []
    for pair in range(4):
        columns = jnp.concatenate([blocks[pair], blocks[8 - pair if pair else 4]], axis=1)
        outs.append(halves(split_dot(columns, table_ref, pair)))
    (p0, p4), (c1, q1), (c2, q2), (c3, q3) = outs
    even, odd = p0 + p4, p0 - p4
    m = diagonal * (c1 - c3)
    n = diagonal * (q1 + q3)
    both, other = c1 + c3, q1 - q3
    return [
        (even + c2) + both,
        (odd - q2) + (m - n),
        (even - c2) - other,
        (odd + q2) - (m + n),
        (even + c2) - both,
        (odd - q2) - (m - n),
        (even - c2) + other,
        (odd + q2) + (m + n),
    ]


def coefficients(diffusivity_ref, s):
    matrix = radau_matrix()
    d = diffusivity_ref[s]
    inverse, coef = [], []
    for i, row in enumerate(matrix):
        inverse.append(1.0 / (1.0 + (6.0 * step_size * row[i]) * d))
        coef.append([(step_size * entry) * d * inverse[i] for entry in row])
    return inverse, coef


def far_layer(n_z):
    return lax.axis_index("gz") % 2 * (n_z - 1)


def far_row(rows):
    return lax.axis_index("xy") % 2 * (rows - 1)


def pack_kernel(
    conc_hbm, pot_hbm, z_far_ref, z_near_ref, x_near_ref, x_far_ref, sems
):
    n_section, n_species, depth, rows, _ = conc_hbm.shape
    z_far = far_layer(depth)
    x_far = far_row(rows)
    layers = ((z_far, z_far_ref), (depth - 1 - z_far, z_near_ref))
    copies = []
    for j in range(n_section):
        copies.append([])
        for q, (z, ref) in enumerate(layers):
            copies[j] += [
                pltpu.make_async_copy(
                    conc_hbm.at[j, :, z], ref.at[j, 0:n_species], sems.at[q, j, 0]
                ),
                pltpu.make_async_copy(pot_hbm.at[j, z], ref.at[j, n_species], sems.at[q, j, 1]),
            ]
        for copy in copies[j]:
            copy.start()
    for j in range(n_section):
        for copy in copies[j]:
            copy.wait()
        for x, out_ref in ((x_far, x_far_ref), (rows - 1 - x_far, x_near_ref)):
            for q, (_, ref) in enumerate(layers):
                for s in range(n_species + 1):
                    to = edge_row(n_section, n_species, depth, j, s, q)
                    out_ref[to : to + 1, :] = ref[j, s, pl.ds(x, 1), :]


def edge_row(n_section, n_species, depth, j, s, q):
    if s < n_species:
        return (j * n_species + s) * depth + q
    return (n_section * n_species + j) * depth + q


def inner_kernel(
    diffusivity_ref, charge_ref, prev_ref, z_far_ref, z_near_ref, wave_ref,
    out_ref, rhs_ref, decay_ref, own_ref, step_ref, between_ref,
):
    n_section, n_species, depth, rows, y_cells = out_ref.shape
    row = lax.broadcasted_iota(jnp.int32, (rows, y_cells), 0)
    layers = (z_far_ref, z_near_ref)
    z_far = far_layer(depth)
    for j in range(n_section):
        for q, ref in enumerate(layers):
            p = ref[j, n_species]
            step_ref[j, q, 0] = p - pltpu.roll(p, 1, 0)
            step_ref[j, q, 1] = pltpu.roll(p, y_cells - 1, 1) - p
            rhs_ref[j, q] = screening * p
        between_ref[j] = z_near_ref[j, n_species] - z_far_ref[j, n_species]

    def species(s, carry):
        half = 0.5 * charge_ref[s].astype(jnp.float32)
        inverse, coef = coefficients(diffusivity_ref, s)
        totals = []
        for j in range(n_section):
            planes = []
            for q, ref in enumerate(layers):
                c = ref[j, s]
                low = face(pltpu.roll(c, 1, 0), c, half * step_ref[j, q, 0])
                low = jnp.where(row == 0, 0.0, low)
                ahead = face(c, pltpu.roll(c, y_cells - 1, 1), half * step_ref[j, q, 1])
                planes.append(
                    (pltpu.roll(low, rows - 1, 0) - low) + (ahead - pltpu.roll(ahead, 1, 1))
                )
            between = face(z_far_ref[j, s], z_near_ref[j, s], half * between_ref[j])
            totals.append((planes[0] + between, planes[1] - between))
        for q, z in enumerate((z_far, depth - 1 - z_far)):
            prev = prev_ref[s, z]
            for i in range(n_section):
                c = layers[q][i, s]
                update = inverse[i] * (prev - c)
                for j in range(n_section):
                    update = update + coef[i][j] * totals[j][q]
                update = c + update
                out_ref[i, s, q] = update
                rhs_ref[i, q] += (2.0 * half) * update
        return carry

    lax.fori_loop(0, n_species, species, 0)
    k1 = wave_ref.shape[0] - decay_ref.shape[1]
    lam = screening + wave_ref[pl.ds(lax.axis_index("gz"), 1), :] + wave_ref[k1:, :]
    root = jnp.sqrt(lam + 0.25 * lam * lam)
    r = 1.0 / (1.0 + 0.5 * lam + root)
    decay_ref[0] = r
    decay_ref[1] = 0.5 / root
    decay_ref[2] = power(r, rows)
    index = lax.axis_index("xy")
    solver = index // ring * group + index % group
    rho = decay_ref[2, pl.ds(solver, 1), :]
    own_ref[0:1, :] = rho
    own_ref[1:2, :] = 1.0 / (1.0 - power(rho, lax.axis_size("xy")))


def outer_kernel(
    diffusivity_ref, charge_ref, part_ref, rhs_part_ref, z_far_ref, z_near_ref, z_far_got,
    x_far_sent, x_far_got, x_near_sent, x_near_got, z_near_got, table_ref,
    out_ref, modes_ref, rhs_ref, edge_ref, step_ref,
):
    n_section, n_species, depth, rows, y_cells = part_ref.shape
    planes = n_species * depth
    pairs = ((z_far_ref, z_far_got), (z_near_ref, z_near_got))
    charge = [charge_ref[s].astype(jnp.float32) for s in range(n_species)]
    kind = lax.broadcasted_iota(jnp.int32, (planes, y_cells), 0) // depth
    by_row = [coefficients(diffusivity_ref, s)[1] for s in range(n_species)]
    z_far = far_layer(depth)
    x_far = far_row(rows)

    def by_species(values):
        total = jnp.full((planes, y_cells), values[0], jnp.float32)
        for s in range(1, n_species):
            total = jnp.where(kind == s, values[s], total)
        return total

    for i in range(n_section):
        for q, (own, got) in enumerate(pairs):
            step_ref[i, q] = got[i, n_species] - own[i, n_species]
            rhs_ref[i, q] = rhs_part_ref[i, q]
    charge_rows = by_species(charge)
    sides = ((x_near_sent, x_near_got), (x_far_sent, x_far_got))
    faces = []
    for near, far in sides:
        for j in range(n_section):
            base = n_section * planes + j * depth
            step = far[base : base + depth, :] - near[base : base + depth, :]
            step = jnp.concatenate([step] * n_species, axis=0)
            at = slice(j * planes, (j + 1) * planes)
            faces.append(face(near[at, :], far[at, :], 0.5 * charge_rows * step))
    edge_rows = (rows - 1 - x_far, x_far)
    for i in range(n_section):
        weights = [by_species([by_row[s][i][j] for s in range(n_species)]) for j in range(n_section)]
        for side, x in enumerate(edge_rows):
            update = weights[0] * faces[side * n_section]
            for j in range(1, n_section):
                update = update + weights[j] * faces[side * n_section + j]
            edge_ref[side, i * planes : (i + 1) * planes, :] = update
            update = charge_rows * update
            total = update[0:depth]
            for s in range(1, n_species):
                total = total + update[s * depth : (s + 1) * depth]
            for q in range(depth):
                rhs_ref[i, q, pl.ds(x, 1), :] += total[q : q + 1]

    def species(s, carry):
        q_s = charge_ref[s].astype(jnp.float32)
        half = 0.5 * q_s
        _, coef = coefficients(diffusivity_ref, s)
        for q, (own, got) in enumerate(pairs):
            faces = [face(own[j, s], got[j, s], half * step_ref[j, q]) for j in range(n_section)]
            for i in range(n_section):
                update = coef[i][0] * faces[0]
                for j in range(1, n_section):
                    update = update + coef[i][j] * faces[j]
                z = z_far if q == 0 else depth - 1 - z_far
                out_ref[i, s, z] = part_ref[i, s, q] + update
                rhs_ref[i, q] += q_s * update
                at = pl.ds((i * n_species + s) * depth + q, 1)
                for side, x in enumerate(edge_rows):
                    out_ref[i, s, z, pl.ds(x, 1), :] += edge_ref[side, at, :]
        return carry

    lax.fori_loop(0, n_species, species, 0)
    rhs = rhs_ref[...].reshape(n_section * depth * rows, y_cells)
    for g, block in enumerate(to_modes(rhs, table_ref)):
        modes_ref[g] = block


def layer_of(z, n_z):
    g = z // n_z
    return g, int(z % n_z != g % 2 * (n_z - 1))


def sine_rows(planes, table):
    depth = len(planes)
    half = depth // 2
    even = [planes[z] + planes[depth - 1 - z] for z in range(half)]
    odd = [planes[z] - planes[depth - 1 - z] for z in range(half)]
    out = []
    for k in range(depth):
        source = even if k % 2 == 0 else odd
        total = source[0] * float(table[k, 0])
        for z in range(1, half):
            total = total + source[z] * float(table[k, z])
        out.append(total)
    return out


def sine_rows_back(planes, table):
    depth = len(planes)
    out = [None] * depth
    for z in range(depth // 2):
        parts = []
        for parity in range(2):
            total = planes[parity] * float(table[parity, z])
            for k in range(parity + 2, depth, 2):
                total = total + planes[k] * float(table[k, z])
            parts.append(total)
        out[z] = parts[0] + parts[1]
        out[depth - 1 - z] = parts[0] - parts[1]
    return out


def sum_kernel(table, decay_ref, modes_ref, hat_ref, sums_ref, rows_ref):
    n_gz, n_section, n_z, rows, _ = modes_ref.shape
    depth = n_gz * n_z
    r = decay_ref[0]
    where = [layer_of(z, n_z) for z in range(depth)]
    for i in range(n_section):
        planes = [modes_ref[g, i, q] for g, q in where]
        for k, plane in enumerate(sine_rows(planes, table)):
            rows_ref[i, pl.ds(k * rows, rows), :] = plane
        for x in range(rows):
            hat_ref[i, x] = rows_ref[i, pl.ds(x, depth, stride=rows), :]
        ahead = hat_ref[i, 0]
        back = hat_ref[i, rows - 1]
        for x in range(1, rows):
            ahead = ahead * r + hat_ref[i, x]
            back = back * r + hat_ref[i, rows - 1 - x]
        for side, value in enumerate((ahead, back)):
            at = side * n_section + i
            for y in range(depth // group):
                four = value[y * group : (y + 1) * group]
                for copy in range(ring // group):
                    first = (y * ring + copy * group) * 2 * n_section + at
                    sums_ref[pl.ds(first, group, stride=2 * n_section), :] = four


def ring_kernel(n_section, own_ref, sums_ref, out_ref, all_ref):
    per = 2 * n_section
    n_rings = sums_ref.shape[0] // (per * ring)
    rho = jnp.broadcast_to(own_ref[0:1, :], (n_section, lanes))
    around = power(rho, ring)
    scale = own_ref[1:2, :]

    def ahead_sum(y, z):
        at = (y * ring + z) * per
        return sums_ref[at : at + n_section, :]

    def back_sum(y, z):
        at = (y * ring + z) * per + n_section
        return sums_ref[at : at + n_section, :]

    ahead, back = [], []
    for y in range(n_rings):
        forth, aback = ahead_sum(y, 0), back_sum(y, ring - 1)
        for z in range(1, ring):
            forth = forth * rho + ahead_sum(y, z)
            aback = aback * rho + back_sum(y, ring - 1 - z)
        ahead.append(forth)
        back.append(aback)
    for y in range(n_rings):
        forth, aback = ahead[y], back[y]
        for distance in range(n_rings - 1, 0, -1):
            forth = forth * around + ahead[(y - distance) % n_rings]
            aback = aback * around + back[(y + distance) % n_rings]
        forth, aback = forth * scale, aback * scale
        for z in range(ring):
            at = (y * ring + z) * per
            all_ref[at : at + n_section, :] = forth
            forth = forth * rho + ahead_sum(y, z)
            e = ring - 1 - z
            at = (y * ring + e) * per + n_section
            all_ref[at : at + n_section, :] = aback
            aback = aback * rho + back_sum(y, e)
    mine = lax.axis_index("xy") % ring // group
    span = group * per
    for y in range(n_rings):
        first = pl.multiple_of(y * ring * per + mine * span, 8)
        out_ref[y * span : (y + 1) * span, :] = all_ref[pl.ds(first, span), :]


def solve_kernel(table, decay_ref, hat_ref, enter_ref, out_ref, work_ref, rows_ref):
    n_gz, n_section, n_z, rows, _ = out_ref.shape
    depth = n_gz * n_z
    r = decay_ref[0]
    inverse = decay_ref[1]
    where = [layer_of(z, n_z) for z in range(depth)]
    for i in range(n_section):
        value = enter_ref[pl.ds(i, depth, stride=2 * n_section), :]
        for x in range(rows):
            source = hat_ref[i, x]
            work_ref[x] = value * r
            value = value * r + source
        value = enter_ref[pl.ds(n_section + i, depth, stride=2 * n_section), :]
        for x in range(rows - 1, -1, -1):
            value = value * r + hat_ref[i, x]
            rows_ref[i, pl.ds(x, depth, stride=rows), :] = (work_ref[x] + value) * inverse
        planes = [rows_ref[i, pl.ds(k * rows, rows), :] for k in range(depth)]
        for (g, q), plane in zip(where, sine_rows_back(planes, table)):
            out_ref[g, i, q] = plane


def final_kernel(solved_ref, table_ref, conc_ref, out_hbm, conc_hbm, out_ref, sems, conc_sem):
    conc_copy = pltpu.make_async_copy(conc_ref, conc_hbm, conc_sem)
    conc_copy.start()
    n_gz, n_section, n_z, rows, _ = solved_ref.shape
    z_far = far_layer(n_z)
    blocks = [solved_ref[g].reshape(n_section * n_z * rows, lanes) for g in range(n_gz)]
    fields = from_modes(blocks, table_ref)
    copies = []
    for i in range(n_section):
        for q, z in enumerate((z_far, n_z - 1 - z_far)):
            at = (i * n_z + q) * rows
            for a, field in enumerate(fields):
                out_ref[i, q, :, a * lanes : (a + 1) * lanes] = field[at : at + rows]
            copies.append(
                pltpu.make_async_copy(out_ref.at[i, q], out_hbm.at[i, z], sems.at[i, q])
            )
            copies[-1].start()
    for copy in copies:
        copy.wait()
    conc_copy.wait()


def on_device(conc_prev, conc_section, potential, diffusivity, charges):
    n_xy = lax.axis_size("xy")
    n_gz = lax.axis_size("gz")
    n_section, n_species, n_z, rows, y_cells = conc_section.shape
    depth = n_z * n_gz
    f32 = jnp.float32
    vmem = pl.BlockSpec(memory_space=pltpu.VMEM)
    smem = pl.BlockSpec(memory_space=pltpu.SMEM)
    hbm = pl.BlockSpec(memory_space=pltpu.HBM)

    def params(mib):
        return pltpu.CompilerParams(vmem_limit_bytes=mib * 1024 * 1024)

    tables = hartley_tables(y_cells)
    table, table_back = jnp.asarray(tables), jnp.asarray(tables.swapaxes(2, 3))
    sine = sine_matrix(depth)
    wave = jnp.asarray(wave_table(depth, y_cells))

    layers = jax.ShapeDtypeStruct((n_section, n_species + 1, rows, y_cells), f32)
    edges = jax.ShapeDtypeStruct((n_section * n_z * (n_species + 1), y_cells), f32)
    z_far_out, z_near_out, x_near_out, x_far_out = pl.pallas_call(
        pack_kernel,
        out_shape=(layers, layers, edges, edges),
        in_specs=[hbm] * 2,
        out_specs=(vmem,) * 4,
        scratch_shapes=[pltpu.SemaphoreType.DMA((n_z, n_section, 2))],
        compiler_params=params(12),
        name="pack",
    )(
        pltpu.with_memory_space_constraint(conc_section, pltpu.HBM),
        pltpu.with_memory_space_constraint(potential, pltpu.HBM),
    )

    def swap(value, axis, pairs):
        return lax.ppermute(value, axis, pairs + [(j, i) for i, j in pairs])

    z_far_in = swap(z_far_out, "gz", [(i, i + 1) for i in range(1, n_gz - 1, 2)])
    x_far_in = swap(x_far_out, "xy", [(i, (i + 1) % n_xy) for i in range(1, n_xy, 2)])
    x_near_in = swap(x_near_out, "xy", [(i, i + 1) for i in range(0, n_xy, 2)])
    z_near_in = swap(z_near_out, "gz", [(i, i + 1) for i in range(0, n_gz, 2)])

    planes = (n_section, n_species, n_z, rows, y_cells)
    rhs_shape = (n_section, n_z, rows, y_cells)
    part, rhs_part, decay_here, own = pl.pallas_call(
        inner_kernel,
        out_shape=(
            jax.ShapeDtypeStruct(planes, f32),
            jax.ShapeDtypeStruct(rhs_shape, f32),
            jax.ShapeDtypeStruct((3, depth, lanes), f32),
            jax.ShapeDtypeStruct((2, lanes), f32),
        ),
        in_specs=[smem] * 2 + [vmem] * 4,
        out_specs=(vmem,) * 4,
        scratch_shapes=[
            pltpu.VMEM((n_section, n_z, 2, rows, y_cells), f32),
            pltpu.VMEM((n_section, rows, y_cells), f32),
        ],
        compiler_params=params(24),
        cost_estimate=pl.CostEstimate(flops=20_000_000, bytes_accessed=4_500_000, transcendentals=0),
        name="inner_faces",
    )(diffusivity, charges, conc_prev, z_far_out, z_near_out, wave)

    conc_new, modes = pl.pallas_call(
        outer_kernel,
        out_shape=(
            pltpu.VMEM(conc_section.shape, f32),
            jax.ShapeDtypeStruct((n_gz, n_section * n_z * rows, lanes), f32),
        ),
        in_specs=[smem] * 2 + [vmem] * 11,
        out_specs=(vmem, vmem),
        scratch_shapes=[
            pltpu.VMEM(rhs_shape, f32),
            pltpu.VMEM((2, n_section * n_species * n_z, y_cells), f32),
            pltpu.VMEM(rhs_shape, f32),
        ],
        compiler_params=params(24),
        name="outer_faces",
    )(
        diffusivity, charges, part, rhs_part, z_far_out, z_near_out, z_far_in,
        x_far_out, x_far_in, x_near_out, x_near_in, z_near_in, table,
    )

    columns = lax.all_to_all(modes, "gz", split_axis=0, concat_axis=0, tiled=True)
    columns = columns.reshape(n_gz, n_section, n_z, rows, lanes)

    n_rows = 2 * n_section * n_xy
    hat, sums = pl.pallas_call(
        functools.partial(sum_kernel, sine),
        out_shape=(
            jax.ShapeDtypeStruct((n_section, rows, depth, lanes), f32),
            jax.ShapeDtypeStruct((n_rows, lanes), f32),
        ),
        in_specs=[vmem] * 2,
        out_specs=(vmem, vmem),
        scratch_shapes=[pltpu.VMEM((n_section, depth * rows, lanes), f32)],
        compiler_params=params(12),
        name="block_sums",
    )(decay_here, columns)

    sums = sums.reshape(n_xy, n_section, 2, lanes)
    gathered = lax.all_to_all(sums, "xy", split_axis=0, concat_axis=0, tiled=True)
    gathered = gathered.reshape(n_rows, lanes)
    entering = pl.pallas_call(
        functools.partial(ring_kernel, n_section),
        out_shape=jax.ShapeDtypeStruct((2 * n_section * depth, lanes), f32),
        in_specs=[vmem] * 2,
        out_specs=vmem,
        scratch_shapes=[pltpu.VMEM((n_rows, lanes), f32)],
        compiler_params=params(12),
        name="ring",
    )(own, gathered)
    sharers = [
        [y * ring + first + z for y in range(n_xy // ring) for z in range(group)]
        for first in range(0, ring, group)
    ]
    entering = entering.reshape(depth, n_section, 2, lanes)
    enter = lax.all_to_all(
        entering, "xy", split_axis=0, concat_axis=0, tiled=True, axis_index_groups=sharers
    )
    enter = enter.reshape(2 * n_section * depth, lanes)

    solved = pl.pallas_call(
        functools.partial(solve_kernel, sine),
        out_shape=jax.ShapeDtypeStruct((n_gz, n_section, n_z, rows, lanes), f32),
        in_specs=[vmem] * 3,
        out_specs=vmem,
        scratch_shapes=[
            pltpu.VMEM((rows, depth, lanes), f32),
            pltpu.VMEM((n_section, depth * rows, lanes), f32),
        ],
        compiler_params=params(12),
        name="solve",
    )(decay_here, hat, enter)
    returned = lax.all_to_all(solved, "gz", split_axis=0, concat_axis=0, tiled=True)

    potential_new, conc_new = pl.pallas_call(
        final_kernel,
        out_shape=(
            jax.ShapeDtypeStruct(potential.shape, f32),
            jax.ShapeDtypeStruct(conc_section.shape, f32),
        ),
        in_specs=[vmem] * 3,
        out_specs=(hbm, hbm),
        scratch_shapes=[
            pltpu.VMEM(potential.shape, f32),
            pltpu.SemaphoreType.DMA((n_section, n_z)),
            pltpu.SemaphoreType.DMA(()),
        ],
        compiler_params=params(12),
        name="back_to_y",
    )(returned, table_back, conc_new)
    return (conc_new, potential_new)


def solution(mesh):
    in_specs = (
        P(None, "gz", "xy", None),
        P(None, None, "gz", "xy", None),
        P(None, "gz", "xy", None),
        P(),
        P(),
    )
    out_specs = (P(None, None, "gz", "xy", None), P(None, "gz", "xy", None))
    return jax.shard_map(
        on_device, mesh=mesh, in_specs=in_specs, out_specs=out_specs, check_vma=False
    )
```

```python
import functools
import math

import jax
import jax.numpy as jnp
import numpy as np
from jax import lax
from jax.experimental import pallas as pl
from jax.experimental.pallas import tpu as pltpu
from jax.sharding import PartitionSpec as P

step_size = 0.2
screening = 0.005
lanes = 128
ring = 16
group = 4
diagonal = math.sqrt(0.5)


def radau_matrix():
    root = math.sqrt(6.0)
    return [
        [(88.0 - 7.0 * root) / 360.0, (296.0 - 169.0 * root) / 1800.0, (-2.0 + 3.0 * root) / 225.0],
        [(296.0 + 169.0 * root) / 1800.0, (88.0 + 7.0 * root) / 360.0, (-2.0 - 3.0 * root) / 225.0],
        [(16.0 - root) / 36.0, (16.0 + root) / 36.0, 1.0 / 9.0],
    ]


def hartley_tables(length):
    b = np.arange(lanes)
    k1 = np.arange(length // lanes)[:, None, None]
    angle = b[:, None] * (k1 + length // lanes * b[None, :]) % length * (2.0 * math.pi / length)
    cas, dif = np.cos(angle) + np.sin(angle), np.sin(angle) - np.cos(angle)
    zero = np.zeros((lanes, lanes))
    pairs = [np.block([[cas[0], zero], [zero, cas[4]]])]
    pairs += [np.block([[cas[p], cas[8 - p]], [dif[p], -dif[8 - p]]]) for p in (1, 2, 3)]
    table = (np.stack(pairs) / math.sqrt(length)).astype(np.float32)
    high = table.astype(jnp.bfloat16)
    low = (table - high.astype(np.float32)).astype(jnp.bfloat16)
    return np.stack([high, low])


def sine_matrix(depth):
    k = np.arange(1, depth + 1)
    return math.sqrt(2.0 / (depth + 1)) * np.sin(np.outer(k, k) * math.pi / (depth + 1))


def wave_table(depth, y_cells):
    k1 = y_cells // lanes
    ky = np.arange(k1)[:, None] + k1 * np.arange(lanes)[None, :]
    ey = 2.0 - 2.0 * np.cos(ky * 2.0 * math.pi / y_cells)
    ez = 2.0 - 2.0 * np.cos(np.arange(1, depth + 1) * math.pi / (depth + 1))
    return np.concatenate([ey, np.broadcast_to(ez[:, None], (depth, lanes))]).astype(np.float32)


def power(value, exponent):
    for _ in range(exponent.bit_length() - 1):
        value = value * value
    return value


def face(near, far, gain):
    return (far - near) + gain * (near + far)


def split_dot(rows, table_ref, pair):
    count = rows.shape[0]
    high = rows.astype(jnp.bfloat16)
    low = (rows - high.astype(jnp.float32)).astype(jnp.bfloat16)

    def product(a, b):
        return jnp.dot(a, b, preferred_element_type=jnp.float32)

    main = product(jnp.concatenate([low, high], axis=0), table_ref[0, pair])
    return (product(high, table_ref[1, pair]) + main[:count]) + main[count:]


def halves(value):
    return value[:, :lanes], value[:, lanes:]


def to_modes(rhs, table_ref):
    f = [rhs[:, a * lanes : (a + 1) * lanes] for a in range(8)]
    s = [f[a] + f[a + 4] for a in range(4)]
    d = [f[a] - f[a + 4] for a in range(4)]
    u = diagonal * (d[1] - d[3])
    v = diagonal * (d[1] + d[3])
    even, odd = s[0] + s[2], s[1] + s[3]
    inputs = [
        (even + odd, even - odd),
        (d[0] + u, -(d[2] + v)),
        (s[0] - s[2], s[3] - s[1]),
        (d[0] - u, d[2] - v),
    ]
    blocks = [None] * 8
    for pair, columns in enumerate(inputs):
        out = split_dot(jnp.concatenate(columns, axis=1), table_ref, pair)
        blocks[pair], blocks[8 - pair if pair else 4] = halves(out)
    return blocks


def from_modes(blocks, table_ref):
    outs = []
    for pair in range(4):
        columns = jnp.concatenate([blocks[pair], blocks[8 - pair if pair else 4]], axis=1)
        outs.append(halves(split_dot(columns, table_ref, pair)))
    (p0, p4), (c1, q1), (c2, q2), (c3, q3) = outs
    even, odd = p0 + p4, p0 - p4
    m = diagonal * (c1 - c3)
    n = diagonal * (q1 + q3)
    both, other = c1 + c3, q1 - q3
    return [
        (even + c2) + both,
        (odd - q2) + (m - n),
        (even - c2) - other,
        (odd + q2) - (m + n),
        (even + c2) - both,
        (odd - q2) - (m - n),
        (even - c2) + other,
        (odd + q2) + (m + n),
    ]


def coefficients(diffusivity_ref, s):
    matrix = radau_matrix()
    d = diffusivity_ref[s]
    inverse, coef = [], []
    for i, row in enumerate(matrix):
        inverse.append(1.0 / (1.0 + (6.0 * step_size * row[i]) * d))
        coef.append([(step_size * entry) * d * inverse[i] for entry in row])
    return inverse, coef


def far_layer(n_z):
    return lax.axis_index("gz") % 2 * (n_z - 1)


def far_row(rows):
    return lax.axis_index("xy") % 2 * (rows - 1)


def pack_kernel(
    conc_hbm, pot_hbm, z_far_ref, z_near_ref, x_near_ref, x_far_ref, sems
):
    n_section, n_species, depth, rows, _ = conc_hbm.shape
    z_far = far_layer(depth)
    x_far = far_row(rows)
    layers = ((z_far, z_far_ref), (depth - 1 - z_far, z_near_ref))
    copies = []
    for j in range(n_section):
        copies.append([])
        for q, (z, ref) in enumerate(layers):
            copies[j] += [
                pltpu.make_async_copy(
                    conc_hbm.at[j, :, z], ref.at[j, 0:n_species], sems.at[q, j, 0]
                ),
                pltpu.make_async_copy(pot_hbm.at[j, z], ref.at[j, n_species], sems.at[q, j, 1]),
            ]
        for copy in copies[j]:
            copy.start()
    for j in range(n_section):
        for copy in copies[j]:
            copy.wait()
        for x, out_ref in ((x_far, x_far_ref), (rows - 1 - x_far, x_near_ref)):
            for q, (_, ref) in enumerate(layers):
                for s in range(n_species + 1):
                    to = edge_row(n_section, n_species, depth, j, s, q)
                    out_ref[to : to + 1, :] = ref[j, s, pl.ds(x, 1), :]


def edge_row(n_section, n_species, depth, j, s, q):
    if s < n_species:
        return (j * n_species + s) * depth + q
    return (n_section * n_species + j) * depth + q


def inner_kernel(
    diffusivity_ref, charge_ref, prev_ref, z_far_ref, z_near_ref, wave_ref,
    out_ref, rhs_ref, decay_ref, own_ref, step_ref, between_ref,
):
    n_section, n_species, depth, rows, y_cells = out_ref.shape
    row = lax.broadcasted_iota(jnp.int32, (rows, y_cells), 0)
    layers = (z_far_ref, z_near_ref)
    z_far = far_layer(depth)
    for j in range(n_section):
        for q, ref in enumerate(layers):
            p = ref[j, n_species]
            step_ref[j, q, 0] = p - pltpu.roll(p, 1, 0)
            step_ref[j, q, 1] = pltpu.roll(p, y_cells - 1, 1) - p
            rhs_ref[j, q] = screening * p
        between_ref[j] = z_near_ref[j, n_species] - z_far_ref[j, n_species]

    def species(s, carry):
        half = 0.5 * charge_ref[s].astype(jnp.float32)
        inverse, coef = coefficients(diffusivity_ref, s)
        totals = []
        for j in range(n_section):
            planes = []
            for q, ref in enumerate(layers):
                c = ref[j, s]
                low = face(pltpu.roll(c, 1, 0), c, half * step_ref[j, q, 0])
                low = jnp.where(row == 0, 0.0, low)
                ahead = face(c, pltpu.roll(c, y_cells - 1, 1), half * step_ref[j, q, 1])
                planes.append(
                    (pltpu.roll(low, rows - 1, 0) - low) + (ahead - pltpu.roll(ahead, 1, 1))
                )
            between = face(z_far_ref[j, s], z_near_ref[j, s], half * between_ref[j])
            totals.append((planes[0] + between, planes[1] - between))
        for q, z in enumerate((z_far, depth - 1 - z_far)):
            prev = prev_ref[s, z]
            for i in range(n_section):
                c = layers[q][i, s]
                update = inverse[i] * (prev - c)
                for j in range(n_section):
                    update = update + coef[i][j] * totals[j][q]
                update = c + update
                out_ref[i, s, q] = update
                rhs_ref[i, q] += (2.0 * half) * update
        return carry

    lax.fori_loop(0, n_species, species, 0)
    k1 = wave_ref.shape[0] - decay_ref.shape[1]
    lam = screening + wave_ref[pl.ds(lax.axis_index("gz"), 1), :] + wave_ref[k1:, :]
    root = jnp.sqrt(lam + 0.25 * lam * lam)
    r = 1.0 / (1.0 + 0.5 * lam + root)
    decay_ref[0] = r
    decay_ref[1] = 0.5 / root
    decay_ref[2] = power(r, rows)
    index = lax.axis_index("xy")
    solver = index // ring * group + index % group
    rho = decay_ref[2, pl.ds(solver, 1), :]
    own_ref[0:1, :] = rho
    own_ref[1:2, :] = 1.0 / (1.0 - power(rho, lax.axis_size("xy")))


def outer_kernel(
    diffusivity_ref, charge_ref, part_ref, rhs_part_ref, z_far_ref, z_near_ref, z_far_got,
    x_far_sent, x_far_got, x_near_sent, x_near_got, z_near_got, table_ref,
    out_ref, modes_ref, rhs_ref, edge_ref, step_ref,
):
    n_section, n_species, depth, rows, y_cells = part_ref.shape
    planes = n_species * depth
    pairs = ((z_far_ref, z_far_got), (z_near_ref, z_near_got))
    charge = [charge_ref[s].astype(jnp.float32) for s in range(n_species)]
    kind = lax.broadcasted_iota(jnp.int32, (planes, y_cells), 0) // depth
    by_row = [coefficients(diffusivity_ref, s)[1] for s in range(n_species)]
    z_far = far_layer(depth)
    x_far = far_row(rows)

    def by_species(values):
        total = jnp.full((planes, y_cells), values[0], jnp.float32)
        for s in range(1, n_species):
            total = jnp.where(kind == s, values[s], total)
        return total

    for i in range(n_section):
        for q, (own, got) in enumerate(pairs):
            step_ref[i, q] = got[i, n_species] - own[i, n_species]
            rhs_ref[i, q] = rhs_part_ref[i, q]
    charge_rows = by_species(charge)
    sides = ((x_near_sent, x_near_got), (x_far_sent, x_far_got))
    faces = []
    for near, far in sides:
        for j in range(n_section):
            base = n_section * planes + j * depth
            step = far[base : base + depth, :] - near[base : base + depth, :]
            step = jnp.concatenate([step] * n_species, axis=0)
            at = slice(j * planes, (j + 1) * planes)
            faces.append(face(near[at, :], far[at, :], 0.5 * charge_rows * step))
    edge_rows = (rows - 1 - x_far, x_far)
    for i in range(n_section):
        weights = [by_species([by_row[s][i][j] for s in range(n_species)]) for j in range(n_section)]
        for side, x in enumerate(edge_rows):
            update = weights[0] * faces[side * n_section]
            for j in range(1, n_section):
                update = update + weights[j] * faces[side * n_section + j]
            edge_ref[side, i * planes : (i + 1) * planes, :] = update
            update = charge_rows * update
            total = update[0:depth]
            for s in range(1, n_species):
                total = total + update[s * depth : (s + 1) * depth]
            for q in range(depth):
                rhs_ref[i, q, pl.ds(x, 1), :] += total[q : q + 1]

    def species(s, carry):
        q_s = charge_ref[s].astype(jnp.float32)
        half = 0.5 * q_s
        _, coef = coefficients(diffusivity_ref, s)
        for q, (own, got) in enumerate(pairs):
            faces = [face(own[j, s], got[j, s], half * step_ref[j, q]) for j in range(n_section)]
            for i in range(n_section):
                update = coef[i][0] * faces[0]
                for j in range(1, n_section):
                    update = update + coef[i][j] * faces[j]
                z = z_far if q == 0 else depth - 1 - z_far
                out_ref[i, s, z] = part_ref[i, s, q] + update
                rhs_ref[i, q] += q_s * update
                at = pl.ds((i * n_species + s) * depth + q, 1)
                for side, x in enumerate(edge_rows):
                    out_ref[i, s, z, pl.ds(x, 1), :] += edge_ref[side, at, :]
        return carry

    lax.fori_loop(0, n_species, species, 0)
    rhs = rhs_ref[...].reshape(n_section * depth * rows, y_cells)
    for g, block in enumerate(to_modes(rhs, table_ref)):
        modes_ref[g] = block


def layer_of(z, n_z):
    g = z // n_z
    return g, int(z % n_z != g % 2 * (n_z - 1))


def sine_rows(planes, table):
    depth = len(planes)
    half = depth // 2
    even = [planes[z] + planes[depth - 1 - z] for z in range(half)]
    odd = [planes[z] - planes[depth - 1 - z] for z in range(half)]
    out = []
    for k in range(depth):
        source = even if k % 2 == 0 else odd
        total = source[0] * float(table[k, 0])
        for z in range(1, half):
            total = total + source[z] * float(table[k, z])
        out.append(total)
    return out


def sine_rows_back(planes, table):
    depth = len(planes)
    out = [None] * depth
    for z in range(depth // 2):
        parts = []
        for parity in range(2):
            total = planes[parity] * float(table[parity, z])
            for k in range(parity + 2, depth, 2):
                total = total + planes[k] * float(table[k, z])
            parts.append(total)
        out[z] = parts[0] + parts[1]
        out[depth - 1 - z] = parts[0] - parts[1]
    return out


def sum_kernel(table, decay_ref, modes_ref, hat_ref, sums_ref, rows_ref):
    n_gz, n_section, n_z, rows, _ = modes_ref.shape
    depth = n_gz * n_z
    r = decay_ref[0]
    where = [layer_of(z, n_z) for z in range(depth)]
    for i in range(n_section):
        planes = [modes_ref[g, i, q] for g, q in where]
        for k, plane in enumerate(sine_rows(planes, table)):
            rows_ref[i, pl.ds(k * rows, rows), :] = plane
        for x in range(rows):
            hat_ref[i, x] = rows_ref[i, pl.ds(x, depth, stride=rows), :]
        ahead = hat_ref[i, 0]
        back = hat_ref[i, rows - 1]
        for x in range(1, rows):
            ahead = ahead * r + hat_ref[i, x]
            back = back * r + hat_ref[i, rows - 1 - x]
        for side, value in enumerate((ahead, back)):
            at = side * n_section + i
            for y in range(depth // group):
                four = value[y * group : (y + 1) * group]
                for copy in range(ring // group):
                    first = (y * ring + copy * group) * 2 * n_section + at
                    sums_ref[pl.ds(first, group, stride=2 * n_section), :] = four


def ring_kernel(n_section, own_ref, sums_ref, out_ref, all_ref):
    per = 2 * n_section
    n_rings = sums_ref.shape[0] // (per * ring)
    rho = jnp.broadcast_to(own_ref[0:1, :], (n_section, lanes))
    around = power(rho, ring)
    scale = own_ref[1:2, :]

    def ahead_sum(y, z):
        at = (y * ring + z) * per
        return sums_ref[at : at + n_section, :]

    def back_sum(y, z):
        at = (y * ring + z) * per + n_section
        return sums_ref[at : at + n_section, :]

    ahead, back = [], []
    for y in range(n_rings):
        forth, aback = ahead_sum(y, 0), back_sum(y, ring - 1)
        for z in range(1, ring):
            forth = forth * rho + ahead_sum(y, z)
            aback = aback * rho + back_sum(y, ring - 1 - z)
        ahead.append(forth)
        back.append(aback)
    for y in range(n_rings):
        forth, aback = ahead[y], back[y]
        for distance in range(n_rings - 1, 0, -1):
            forth = forth * around + ahead[(y - distance) % n_rings]
            aback = aback * around + back[(y + distance) % n_rings]
        forth, aback = forth * scale, aback * scale
        for z in range(ring):
            at = (y * ring + z) * per
            all_ref[at : at + n_section, :] = forth
            forth = forth * rho + ahead_sum(y, z)
            e = ring - 1 - z
            at = (y * ring + e) * per + n_section
            all_ref[at : at + n_section, :] = aback
            aback = aback * rho + back_sum(y, e)
    mine = lax.axis_index("xy") % ring // group
    span = group * per
    for y in range(n_rings):
        first = pl.multiple_of(y * ring * per + mine * span, 8)
        out_ref[y * span : (y + 1) * span, :] = all_ref[pl.ds(first, span), :]


def solve_kernel(
    table, decay_ref, hat_ref, enter_ref, conc_ref, out_ref, conc_hbm, work_ref, rows_ref, sem
):
    n_gz, n_section, n_z, rows, _ = out_ref.shape
    conc_copy = pltpu.make_async_copy(conc_ref.at[0], conc_hbm.at[0], sem)
    conc_copy.start()
    depth = n_gz * n_z
    r = decay_ref[0]
    inverse = decay_ref[1]
    where = [layer_of(z, n_z) for z in range(depth)]
    for i in range(n_section):
        value = enter_ref[pl.ds(i, depth, stride=2 * n_section), :]
        for x in range(rows):
            source = hat_ref[i, x]
            work_ref[x] = value * r
            value = value * r + source
        value = enter_ref[pl.ds(n_section + i, depth, stride=2 * n_section), :]
        for x in range(rows - 1, -1, -1):
            value = value * r + hat_ref[i, x]
            rows_ref[i, pl.ds(x, depth, stride=rows), :] = (work_ref[x] + value) * inverse
        planes = [rows_ref[i, pl.ds(k * rows, rows), :] for k in range(depth)]
        for (g, q), plane in zip(where, sine_rows_back(planes, table)):
            out_ref[g, i, q] = plane
    conc_copy.wait()


def final_kernel(
    solved_ref, table_ref, conc_ref, _, out_hbm, conc_hbm, out_ref, sems, conc_sem
):
    rest = pl.ds(1, conc_ref.shape[0] - 1)
    conc_copy = pltpu.make_async_copy(conc_ref.at[rest], conc_hbm.at[rest], conc_sem)
    conc_copy.start()
    n_gz, n_section, n_z, rows, _ = solved_ref.shape
    z_far = far_layer(n_z)
    blocks = [solved_ref[g].reshape(n_section * n_z * rows, lanes) for g in range(n_gz)]
    fields = from_modes(blocks, table_ref)
    copies = []
    for i in range(n_section):
        for q, z in enumerate((z_far, n_z - 1 - z_far)):
            at = (i * n_z + q) * rows
            for a, field in enumerate(fields):
                out_ref[i, q, :, a * lanes : (a + 1) * lanes] = field[at : at + rows]
            copies.append(
                pltpu.make_async_copy(out_ref.at[i, q], out_hbm.at[i, z], sems.at[i, q])
            )
            copies[-1].start()
    for copy in copies:
        copy.wait()
    conc_copy.wait()


def on_device(conc_prev, conc_section, potential, diffusivity, charges):
    n_xy = lax.axis_size("xy")
    n_gz = lax.axis_size("gz")
    n_section, n_species, n_z, rows, y_cells = conc_section.shape
    depth = n_z * n_gz
    f32 = jnp.float32
    vmem = pl.BlockSpec(memory_space=pltpu.VMEM)
    smem = pl.BlockSpec(memory_space=pltpu.SMEM)
    hbm = pl.BlockSpec(memory_space=pltpu.HBM)

    def params(mib):
        return pltpu.CompilerParams(vmem_limit_bytes=mib * 1024 * 1024)

    tables = hartley_tables(y_cells)
    table, table_back = jnp.asarray(tables), jnp.asarray(tables.swapaxes(2, 3))
    sine = sine_matrix(depth)
    wave = jnp.asarray(wave_table(depth, y_cells))

    layers = jax.ShapeDtypeStruct((n_section, n_species + 1, rows, y_cells), f32)
    edges = jax.ShapeDtypeStruct((n_section * n_z * (n_species + 1), y_cells), f32)
    z_far_out, z_near_out, x_near_out, x_far_out = pl.pallas_call(
        pack_kernel,
        out_shape=(layers, layers, edges, edges),
        in_specs=[hbm] * 2,
        out_specs=(vmem,) * 4,
        scratch_shapes=[pltpu.SemaphoreType.DMA((n_z, n_section, 2))],
        compiler_params=params(12),
        name="pack",
    )(
        pltpu.with_memory_space_constraint(conc_section, pltpu.HBM),
        pltpu.with_memory_space_constraint(potential, pltpu.HBM),
    )

    def swap(value, axis, pairs):
        return lax.ppermute(value, axis, pairs + [(j, i) for i, j in pairs])

    z_far_in = swap(z_far_out, "gz", [(i, i + 1) for i in range(1, n_gz - 1, 2)])
    x_far_in = swap(x_far_out, "xy", [(i, (i + 1) % n_xy) for i in range(1, n_xy, 2)])
    x_near_in = swap(x_near_out, "xy", [(i, i + 1) for i in range(0, n_xy, 2)])
    z_near_in = swap(z_near_out, "gz", [(i, i + 1) for i in range(0, n_gz, 2)])

    planes = (n_section, n_species, n_z, rows, y_cells)
    rhs_shape = (n_section, n_z, rows, y_cells)
    part, rhs_part, decay_here, own = pl.pallas_call(
        inner_kernel,
        out_shape=(
            jax.ShapeDtypeStruct(planes, f32),
            jax.ShapeDtypeStruct(rhs_shape, f32),
            jax.ShapeDtypeStruct((3, depth, lanes), f32),
            jax.ShapeDtypeStruct((2, lanes), f32),
        ),
        in_specs=[smem] * 2 + [vmem] * 4,
        out_specs=(vmem,) * 4,
        scratch_shapes=[
            pltpu.VMEM((n_section, n_z, 2, rows, y_cells), f32),
            pltpu.VMEM((n_section, rows, y_cells), f32),
        ],
        compiler_params=params(24),
        cost_estimate=pl.CostEstimate(flops=20_000_000, bytes_accessed=4_500_000, transcendentals=0),
        name="inner_faces",
    )(diffusivity, charges, conc_prev, z_far_out, z_near_out, wave)

    conc_new, modes = pl.pallas_call(
        outer_kernel,
        out_shape=(
            pltpu.VMEM(conc_section.shape, f32),
            jax.ShapeDtypeStruct((n_gz, n_section * n_z * rows, lanes), f32),
        ),
        in_specs=[smem] * 2 + [vmem] * 11,
        out_specs=(vmem, vmem),
        scratch_shapes=[
            pltpu.VMEM(rhs_shape, f32),
            pltpu.VMEM((2, n_section * n_species * n_z, y_cells), f32),
            pltpu.VMEM(rhs_shape, f32),
        ],
        compiler_params=params(24),
        name="outer_faces",
    )(
        diffusivity, charges, part, rhs_part, z_far_out, z_near_out, z_far_in,
        x_far_out, x_far_in, x_near_out, x_near_in, z_near_in, table,
    )

    columns = lax.all_to_all(modes, "gz", split_axis=0, concat_axis=0, tiled=True)
    columns = columns.reshape(n_gz, n_section, n_z, rows, lanes)

    n_rows = 2 * n_section * n_xy
    hat, sums = pl.pallas_call(
        functools.partial(sum_kernel, sine),
        out_shape=(
            jax.ShapeDtypeStruct((n_section, rows, depth, lanes), f32),
            jax.ShapeDtypeStruct((n_rows, lanes), f32),
        ),
        in_specs=[vmem] * 2,
        out_specs=(vmem, vmem),
        scratch_shapes=[pltpu.VMEM((n_section, depth * rows, lanes), f32)],
        compiler_params=params(12),
        name="block_sums",
    )(decay_here, columns)

    sums = sums.reshape(n_xy, n_section, 2, lanes)
    gathered = lax.all_to_all(sums, "xy", split_axis=0, concat_axis=0, tiled=True)
    gathered = gathered.reshape(n_rows, lanes)
    entering = pl.pallas_call(
        functools.partial(ring_kernel, n_section),
        out_shape=jax.ShapeDtypeStruct((2 * n_section * depth, lanes), f32),
        in_specs=[vmem] * 2,
        out_specs=vmem,
        scratch_shapes=[pltpu.VMEM((n_rows, lanes), f32)],
        compiler_params=params(12),
        name="ring",
    )(own, gathered)
    sharers = [
        [y * ring + first + z for y in range(n_xy // ring) for z in range(group)]
        for first in range(0, ring, group)
    ]
    entering = entering.reshape(depth, n_section, 2, lanes)
    enter = lax.all_to_all(
        entering, "xy", split_axis=0, concat_axis=0, tiled=True, axis_index_groups=sharers
    )
    enter = enter.reshape(2 * n_section * depth, lanes)

    solved, conc_out = pl.pallas_call(
        functools.partial(solve_kernel, sine),
        out_shape=(
            jax.ShapeDtypeStruct((n_gz, n_section, n_z, rows, lanes), f32),
            jax.ShapeDtypeStruct(conc_section.shape, f32),
        ),
        in_specs=[vmem] * 4,
        out_specs=(vmem, hbm),
        scratch_shapes=[
            pltpu.VMEM((rows, depth, lanes), f32),
            pltpu.VMEM((n_section, depth * rows, lanes), f32),
            pltpu.SemaphoreType.DMA(()),
        ],
        compiler_params=params(12),
        name="solve",
    )(decay_here, hat, enter, conc_new)
    returned = lax.all_to_all(solved, "gz", split_axis=0, concat_axis=0, tiled=True)

    potential_new, conc_new = pl.pallas_call(
        final_kernel,
        out_shape=(
            jax.ShapeDtypeStruct(potential.shape, f32),
            jax.ShapeDtypeStruct(conc_section.shape, f32),
        ),
        in_specs=[vmem] * 3 + [hbm],
        input_output_aliases={3: 1},
        out_specs=(hbm, hbm),
        scratch_shapes=[
            pltpu.VMEM(potential.shape, f32),
            pltpu.SemaphoreType.DMA((n_section, n_z)),
            pltpu.SemaphoreType.DMA(()),
        ],
        compiler_params=params(12),
        name="back_to_y",
    )(returned, table_back, conc_new, conc_out)
    return (conc_new, potential_new)


def solution(mesh):
    in_specs = (
        P(None, "gz", "xy", None),
        P(None, None, "gz", "xy", None),
        P(None, "gz", "xy", None),
        P(),
        P(),
    )
    out_specs = (P(None, None, "gz", "xy", None), P(None, "gz", "xy", None))
    return jax.shard_map(
        on_device, mesh=mesh, in_specs=in_specs, out_specs=out_specs, check_vma=False
    )
```
